32 devices in a mesh: groups: 2 (over x), expert: 16 (over z, y, core).
Axes of the slice: x: 2, y: 2, z: 4, core: 2. Of those that a mesh axis runs over, the one named last changes fastest.
Arguments:
- tokens: bfloat16 [4096, 2048], P(('groups', 'expert')), parts along dimension 0, may hold values from -6 to 6
- grad_out: bfloat16 [4096, 2048], P(('groups', 'expert')), parts along dimension 0, may hold values from -6 to 6
- expert_ids: int32 [4096, 4], P(('groups', 'expert')), parts along dimension 0, may hold values from 0 to 15, all different within a row; in each aligned block of 128 rows (0 to 127, 128 to 255, ...) at most 36 rows name the same one
- combine: float32 [4096, 4], P(('groups', 'expert')), parts along dimension 0, may hold values from 0.05 to 0.6
- frozen_gate: bfloat16 [16, 2048, 768], P('expert'), may hold values from -0.125 to 0.125
- frozen_up: bfloat16 [16, 2048, 768], P('expert'), may hold values from -0.125 to 0.125
- frozen_down: bfloat16 [16, 768, 2048], P('expert'), may hold values from -0.21875 to 0.21875
- adapter_gate_in: bfloat16 [16, 32, 2048], P('expert'), may hold values from -0.125 to 0.125
- adapter_gate_out: bfloat16 [16, 32, 768], P('expert'), may hold values from -1 to 1
- adapter_up_in: bfloat16 [16, 32, 2048], P('expert'), may hold values from -0.125 to 0.125
- adapter_up_out: bfloat16 [16, 32, 768], P('expert'), may hold values from -1 to 1
- adapter_down_in: bfloat16 [16, 32, 768], P('expert'), may hold values from -0.21875 to 0.21875
- adapter_down_out: bfloat16 [16, 32, 2048], P('expert'), may hold values from -1 to 1
Outputs:
- grad_tokens: bfloat16 [4096, 2048], P(('groups', 'expert')), parts along dimension 0
- grad_combine: float32 [4096, 4], P(('groups', 'expert')), parts along dimension 0
- grad_gate_in: float32 [32, 32, 2048], P(('groups', 'expert')), parts along dimension 0
- grad_gate_out: float32 [32, 32, 768], P(('groups', 'expert')), parts along dimension 0
- grad_up_in: float32 [32, 32, 2048], P(('groups', 'expert')), parts along dimension 0
- grad_up_out: float32 [32, 32, 768], P(('groups', 'expert')), parts along dimension 0
- grad_down_in: float32 [32, 32, 768], P(('groups', 'expert')), parts along dimension 0
- grad_down_out: float32 [32, 32, 2048], P(('groups', 'expert')), parts along dimension 0
The draws below stay inside these ranges and needn't reach their ends.
There are 2 independent parts, one for each index of `groups`. The reference program is written for one: setup_inputs(seed, part) draws one part's arguments, and reference() takes and returns one part's arrays. A program takes and returns all parts, laid end to end along the dimension named above; an argument that names none is the same for every part. Nothing has to cross between parts.
Inputs may be any that keep to these rules, and one draw needn't show every extreme that they name: `expert_ids`: in each token's row the 4 experts differ. Among the rows of one device no expert is named more than 36 times, a bound that some block reaches; every expert is named somewhere.
All inputs are finite; a program needn't handle non-finite values.
Results may differ from the reference program's by a relative error of at most 0.017.
Values may be sent and summed in bfloat16 or wider, within the bound.
No kernel may reach another device: no remote copies, remote signals or barrier semaphores. Data moves between devices by JAX's collectives and lax.ppermute only.
A program may use at most 128 MiB of HBM per device.

```python
import math
import jax
import jax.numpy as jnp
import numpy as np
from jax import lax

D = 2048
FF = 768
RANK = 32
TOPK = 4
TOK_DEV = 128
EXPERTS = 16
TOKENS = 2048
CAP = 36
N_EXPERT = 16


def shard_levels(rng, extent, cuts, low, largest):
    loudness = 1.0
    for dim, blocks in cuts:
        steps = jax.random.uniform(jax.random.fold_in(jax.random.fold_in(rng, 6), dim), (blocks,), jnp.float32, low / len(cuts), largest / len(cuts))
        loudness = loudness * jnp.repeat(jnp.exp(steps), extent[dim] // blocks).reshape((-1,) + (1,) * (len(extent) - 1 - dim))
    return loudness


def shared_out(key, own, number, rows, number_of, top, limit, lean):
    sequence = jax.random.permutation(key, number_of)
    crowded, common = shares(number_of, rows * top, limit, lean, True), shares(number_of, rows * top, limit, lean, False)
    places = jnp.arange(number_of)

    def named(lengths, offset_by):
        used = int((lengths > 0).sum())
        fixed = max(1, used // 4)
        shifted = fixed + (places - fixed + offset_by * (used - fixed)) % max(1, number_of - fixed)
        return jnp.zeros((number_of,), jnp.int32).at[sequence[jnp.where(places < fixed, places, shifted)]].set(jnp.asarray(lengths, jnp.int32))

    lengths = jnp.where(number % 4 == 0, named(crowded, number // 4), named(common, number - number // 4 - 1))
    mixed = jax.random.permutation(jax.random.fold_in(own, 3), number_of)
    donor, taker = mixed[0:number_of // 2 * 2:2], mixed[1:number_of // 2 * 2:2]
    slack = jnp.minimum(lengths[donor] - 1, limit - lengths[taker]) // 2
    slack = jnp.where((donor == sequence[0]) | (taker == sequence[0]) | (lengths[taker] == 0), 0, jnp.maximum(slack, 0))
    shifted = jax.random.randint(jax.random.fold_in(own, 4), (number_of // 2,), 0, 1 << 20) % (slack + 1)
    lengths = lengths.at[donor].add(-shifted).at[taker].add(shifted)
    members = jnp.searchsorted(jnp.cumsum(lengths), jnp.arange(rows * top), side="right").astype(jnp.int32)
    listing = members.reshape(top, rows).T
    listing = listing[jax.random.permutation(jax.random.fold_in(own, 1), rows)]
    offset_by = jax.random.randint(jax.random.fold_in(own, 2), (rows, 1), 0, top)
    return jnp.take_along_axis(listing, (jnp.arange(top)[None, :] + offset_by) % top, axis=1)


def shares(number_of, total, reach, slope, full):
    weights = [(1 << 20) // math.isqrt(standing ** slope) + 1 for standing in range(1, number_of + 1)]
    largest = reach if full else min(reach, max(-(-total // number_of), total * weights[0] // sum(weights)))
    least = 1 if total - largest >= number_of - 1 else 0
    holding, rest = [largest] + [least] * (number_of - 1), total - largest - least * (number_of - 1)
    while rest > 0:
        free = [i for i in range(1, number_of) if holding[i] < largest] or [i for i in range(1, number_of) if holding[i] < reach]
        pool, remaining = sum([weights[i] for i in free]), rest
        for i in free:
            addition = min(reach - holding[i], max(1, remaining * weights[i] // pool), rest)
            holding[i] = holding[i] + addition
            rest = rest - addition
    return np.array(holding)


def normal_values(stream_key, dims, width, limit, cuts=(), kind=jnp.bfloat16):
    array = width * jax.random.normal(stream_key, dims, jnp.float32)
    if cuts:
        array = array * shard_levels(stream_key, dims, cuts, -0.22, 0.18)
    return jnp.clip(array, -limit, limit).astype(kind)


def setup_inputs(seed: int = 0, part: int = 0) -> dict:
    seeds = jax.random.split(jax.random.key(seed), 14)
    part_splits = jax.random.split(jax.random.fold_in(seeds[13], part), 14)
    tokens = normal_values(part_splits[0], (TOKENS, D), 1.0, 6.0, ((0, 16),))
    grad_out = normal_values(part_splits[1], (TOKENS, D), 1.0, 6.0, ((0, 16),))
    expert_ids_keys = jax.random.split(jax.random.fold_in(part_splits[2], 1), TOKENS // TOK_DEV)
    expert_ids_turns = jax.random.permutation(jax.random.fold_in(part_splits[2], 3), TOKENS // TOK_DEV)
    expert_ids = jax.vmap(lambda own, number: shared_out(jax.random.fold_in(part_splits[2], 2), own, number, TOK_DEV, EXPERTS, TOPK, CAP, 2))(expert_ids_keys, expert_ids_turns).reshape((TOKENS, TOPK))
    combine = jnp.clip(0.05 + 0.55 * jax.random.uniform(part_splits[3], (TOKENS, TOPK), jnp.float32) ** shard_levels(part_splits[3], (TOKENS, TOPK), ((0, 16),), -0.2, 0.2), 0.05, 0.6)
    frozen_gate = normal_values(seeds[4], (EXPERTS, D, FF), D ** -0.5, 0.125, ((0, 16),))
    frozen_up = normal_values(seeds[5], (EXPERTS, D, FF), D ** -0.5, 0.125, ((0, 16),))
    frozen_down = normal_values(seeds[6], (EXPERTS, FF, D), FF ** -0.5, 0.21875, ((0, 16),))
    adapter_gate_in = normal_values(seeds[7], (EXPERTS, RANK, D), D ** -0.5, 0.125, ((0, 16),))
    adapter_gate_out = normal_values(seeds[8], (EXPERTS, RANK, FF), RANK ** -0.5, 1.0, ((0, 16),))
    adapter_up_in = normal_values(seeds[9], (EXPERTS, RANK, D), D ** -0.5, 0.125, ((0, 16),))
    adapter_up_out = normal_values(seeds[10], (EXPERTS, RANK, FF), RANK ** -0.5, 1.0, ((0, 16),))
    adapter_down_in = normal_values(seeds[11], (EXPERTS, RANK, FF), FF ** -0.5, 0.21875, ((0, 16),))
    adapter_down_out = normal_values(seeds[12], (EXPERTS, RANK, D), RANK ** -0.5, 1.0, ((0, 16),))
    return {"tokens": tokens, "grad_out": grad_out, "expert_ids": expert_ids, "combine": combine, "frozen_gate": frozen_gate, "frozen_up": frozen_up, "frozen_down": frozen_down, "adapter_gate_in": adapter_gate_in, "adapter_gate_out": adapter_gate_out, "adapter_up_in": adapter_up_in, "adapter_up_out": adapter_up_out, "adapter_down_in": adapter_down_in, "adapter_down_out": adapter_down_out}


adapter_scale_factor = 2.0


def expert_forward(input_token_rows, gate_weight_matrix, up_weight_matrix, down_weight_matrix, gate_adapter_input, gate_adapter_output, up_adapter_input, up_adapter_output, down_adapter_input, down_adapter_output):
    lowrank_gate_product = jnp.dot(input_token_rows, gate_adapter_input.T, preferred_element_type=jnp.float32).astype(jnp.bfloat16)
    lowrank_up_product = jnp.dot(input_token_rows, up_adapter_input.T, preferred_element_type=jnp.float32).astype(jnp.bfloat16)
    gate_preactivation = jnp.dot(input_token_rows, gate_weight_matrix, preferred_element_type=jnp.float32) + adapter_scale_factor * jnp.dot(lowrank_gate_product, gate_adapter_output, preferred_element_type=jnp.float32)
    up_preactivation = jnp.dot(input_token_rows, up_weight_matrix, preferred_element_type=jnp.float32) + adapter_scale_factor * jnp.dot(lowrank_up_product, up_adapter_output, preferred_element_type=jnp.float32)
    hidden_activation = (jax.nn.silu(gate_preactivation) * up_preactivation).astype(jnp.bfloat16)
    lowrank_down_product = jnp.dot(hidden_activation, down_adapter_input.T, preferred_element_type=jnp.float32).astype(jnp.bfloat16)
    layer_output = (jnp.dot(hidden_activation, down_weight_matrix, preferred_element_type=jnp.float32) + adapter_scale_factor * jnp.dot(lowrank_down_product, down_adapter_output, preferred_element_type=jnp.float32)).astype(jnp.bfloat16)
    return (lowrank_gate_product, lowrank_up_product, gate_preactivation, up_preactivation, hidden_activation, lowrank_down_product, layer_output)


def expert_backward(input_token_rows, gradient_token_rows, weight_rows, saved, gate_weight_matrix, up_weight_matrix, down_weight_matrix, gate_adapter_input, gate_adapter_output, up_adapter_input, up_adapter_output, down_adapter_input, down_adapter_output):
    lowrank_gate_product, lowrank_up_product, gate_preactivation, up_preactivation, hidden_activation, lowrank_down_product, layer_output = saved
    routing_weight_column = weight_rows[:, None]
    down_projection_backward = (routing_weight_column * jnp.dot(gradient_token_rows, down_adapter_output.T, preferred_element_type=jnp.float32)).astype(jnp.bfloat16)
    weighted_lowrank_product = (routing_weight_column * lowrank_down_product.astype(jnp.float32)).astype(jnp.bfloat16)
    hidden_gradient = routing_weight_column * jnp.dot(gradient_token_rows, down_weight_matrix.T, preferred_element_type=jnp.float32) + adapter_scale_factor * jnp.dot(down_projection_backward, down_adapter_input, preferred_element_type=jnp.float32)
    sigmoid_gate = jax.nn.sigmoid(gate_preactivation)
    gate_activation_gradient = (hidden_gradient * up_preactivation * sigmoid_gate * (1.0 + gate_preactivation * (1.0 - sigmoid_gate))).astype(jnp.bfloat16)
    up_activation_gradient = (hidden_gradient * gate_preactivation * sigmoid_gate).astype(jnp.bfloat16)
    gate_projection_backward = jnp.dot(gate_activation_gradient, gate_adapter_output.T, preferred_element_type=jnp.float32).astype(jnp.bfloat16)
    up_projection_backward = jnp.dot(up_activation_gradient, up_adapter_output.T, preferred_element_type=jnp.float32).astype(jnp.bfloat16)
    input_gradient = jnp.dot(gate_activation_gradient, gate_weight_matrix.T, preferred_element_type=jnp.float32) + jnp.dot(up_activation_gradient, up_weight_matrix.T, preferred_element_type=jnp.float32)
    input_gradient = input_gradient + adapter_scale_factor * (jnp.dot(gate_projection_backward, gate_adapter_input, preferred_element_type=jnp.float32) + jnp.dot(up_projection_backward, up_adapter_input, preferred_element_type=jnp.float32))
    input_gradient = input_gradient.astype(jnp.bfloat16)
    grads = (
        adapter_scale_factor * jnp.dot(gate_projection_backward.T, input_token_rows, preferred_element_type=jnp.float32),
        adapter_scale_factor * jnp.dot(lowrank_gate_product.T, gate_activation_gradient, preferred_element_type=jnp.float32),
        adapter_scale_factor * jnp.dot(up_projection_backward.T, input_token_rows, preferred_element_type=jnp.float32),
        adapter_scale_factor * jnp.dot(lowrank_up_product.T, up_activation_gradient, preferred_element_type=jnp.float32),
        adapter_scale_factor * jnp.dot(down_projection_backward.T, hidden_activation, preferred_element_type=jnp.float32),
        adapter_scale_factor * jnp.dot(weighted_lowrank_product.T, gradient_token_rows, preferred_element_type=jnp.float32),
    )
    return input_gradient, grads


def reference(tokens, grad_out, expert_ids, combine, frozen_gate, frozen_up, frozen_down, adapter_gate_in, adapter_gate_out, adapter_up_in, adapter_up_out, adapter_down_in, adapter_down_out):
    assigned = TOK_DEV * TOPK
    blocks = N_EXPERT
    total = TOKENS * TOPK
    flat_experts = expert_ids.reshape(blocks, assigned).astype(jnp.int32)
    onehot = (flat_experts[:, :, None] == jnp.arange(EXPERTS, dtype=jnp.int32)[None, None, :]).astype(jnp.int32)
    before = jnp.cumsum(onehot, axis=1) - onehot
    slot_index = jnp.sum(before * onehot, axis=2)
    source_block = jnp.arange(blocks, dtype=jnp.int32)[:, None]
    position = flat_experts * (blocks * CAP) + source_block * CAP + slot_index
    slot_table = jnp.full((EXPERTS * blocks * CAP,), total, jnp.int32)
    slot_table = slot_table.at[position.reshape(-1)].set(jnp.arange(total, dtype=jnp.int32))
    slot_table = slot_table.reshape(EXPERTS, blocks * CAP)
    tokens_pad = jnp.concatenate([tokens, jnp.zeros((1, D), tokens.dtype)], axis=0)
    grads_pad = jnp.concatenate([grad_out, jnp.zeros((1, D), grad_out.dtype)], axis=0)
    weights_pad = jnp.concatenate([combine.reshape(total), jnp.zeros((1,), combine.dtype)], axis=0)

    def one_expert(packed):
        rows_table = packed[0]
        matrices = packed[1:]
        source_row = rows_table // TOPK
        input_token_rows = tokens_pad[source_row]
        gradient_token_rows = grads_pad[source_row]
        weight_rows = weights_pad[rows_table]
        saved = expert_forward(input_token_rows, *matrices)
        layer_output = saved[6]
        dots = jnp.sum(gradient_token_rows.astype(jnp.float32) * layer_output.astype(jnp.float32), axis=1)
        input_gradient, grads = expert_backward(input_token_rows, gradient_token_rows, weight_rows, saved, *matrices)
        return (input_gradient, dots) + grads

    results = lax.map(one_expert, (slot_table, frozen_gate, frozen_up, frozen_down, adapter_gate_in, adapter_gate_out, adapter_up_in, adapter_up_out, adapter_down_in, adapter_down_out))
    flat_table = slot_table.reshape(-1)
    assign_grad = jnp.zeros((total + 1, D), results[0].dtype).at[flat_table].set(results[0].reshape(-1, D))
    assign_grad = assign_grad[:total].reshape(TOKENS, TOPK, D)
    grad_tokens = jnp.sum(assign_grad.astype(jnp.float32), axis=1).astype(jnp.bfloat16)
    assign_dots = jnp.zeros((total + 1,), jnp.float32).at[flat_table].set(results[1].reshape(-1))
    grad_combine = assign_dots[:total].reshape(TOKENS, TOPK)
    return (grad_tokens, grad_combine, results[2], results[3], results[4], results[5], results[6], results[7])
```

```python
import functools

import jax
import jax.numpy as jnp
from jax import lax
from jax.experimental import pallas as pl
from jax.experimental.pallas import tpu as pltpu
from jax.sharding import PartitionSpec as P

SCALE = 2.0
PLANE = 4
LANES = 128
F32 = jnp.float32
BF16 = jnp.bfloat16
VMEM_LIMIT = 40 * 1024 * 1024


def nn(a, b):
    return lax.dot_general(a, b, (((1,), (0,)), ((), ())), preferred_element_type=F32)


def nt(a, b):
    return lax.dot_general(a, b, (((1,), (1,)), ((), ())), preferred_element_type=F32)


def two_parts(value):
    high = value.astype(BF16).astype(F32)
    return high, value - high


def vmem():
    return pl.BlockSpec(memory_space=pltpu.VMEM)


def smem():
    return pl.BlockSpec(memory_space=pltpu.SMEM)


def anywhere():
    return pl.BlockSpec(memory_space=pl.ANY)


def cost(flops, moved, exps=0):
    return pl.CostEstimate(flops=int(flops), bytes_accessed=int(moved), transcendentals=int(exps))


def params():
    return pltpu.CompilerParams(vmem_limit_bytes=VMEM_LIMIT)


def one_hots(names, slots, side, routes):
    turned = side.T
    tokens = side.shape[0]
    earlier = lax.broadcasted_iota(jnp.int32, (tokens, tokens), 0)
    later = lax.broadcasted_iota(jnp.int32, (tokens, tokens), 1)
    ahead = jnp.where(earlier < later, 1.0, 0.0).astype(BF16)
    place = lax.broadcasted_iota(jnp.int32, (slots, tokens), 0).astype(F32)
    found = []
    for name in names:
        hits = [jnp.where(turned[k : k + 1, :] == name, 1.0, 0.0) for k in range(routes)]
        member = sum(hits)
        wide = jnp.broadcast_to(member, (8, tokens)).astype(BF16)
        slot = nn(wide, ahead)[0:1, :]
        found.append((jnp.where((place == slot) & (member > 0.0), 1.0, 0.0), hits))
    return turned, found


def pack_kernel(routes, grad_ref, ids_ref, weight_ref, out_ref):
    width = grad_ref.shape[1]
    out_ref[:, :width] = grad_ref[...]
    names = ids_ref[...].astype(F32) + 1.0
    high, low = two_parts(weight_ref[...])
    lane = lax.broadcasted_iota(jnp.int32, (grad_ref.shape[0], LANES), 1)
    side = jnp.zeros((grad_ref.shape[0], LANES), F32)
    for group, values in enumerate((names, names, high, low)):
        for k in range(routes):
            side = jnp.where(lane == group * routes + k, values[:, k : k + 1], side)
    out_ref[:, width:] = side.astype(BF16)


def select_kernel(routes, slots, choices, info_ref, *refs):
    xs, gs = refs[:choices], refs[choices : 2 * choices]
    outs = refs[2 * choices : 2 * choices + PLANE]
    side_ref, x_buf, g_buf, x_sem, g_sem = refs[2 * choices + PLANE :]
    for i in range(choices):

        @pl.when(info_ref[PLANE] == i)
        def _():
            g_copy = pltpu.make_async_copy(gs[i], g_buf, g_sem)
            x_copy = pltpu.make_async_copy(xs[i], x_buf, x_sem)
            g_copy.start()
            x_copy.start()
            g_copy.wait()
            x_copy.wait()

    width = x_buf.shape[1]
    side_ref[...] = g_buf[:, width:]
    side = g_buf[:, width:].astype(F32)
    names = [info_ref[m].astype(F32) + 1.0 for m in range(PLANE)]
    turned, found = one_hots(names, slots, side, routes)
    lane = lax.broadcasted_iota(jnp.int32, (slots, LANES), 1)
    picks = jnp.concatenate([hot for hot, _ in found], axis=0).astype(BF16)
    x_rows = nn(picks, x_buf[...])
    g_rows = nn(picks, g_buf[:, :width])
    for m, (hot, hits) in enumerate(found):
        rows = slice(m * slots, (m + 1) * slots)
        outs[m][:, :width] = x_rows[rows].astype(BF16)
        outs[m][:, width : 2 * width] = g_rows[rows].astype(BF16)
        parts = []
        for group in (2, 3):
            weight = sum(hits[k] * turned[group * routes + k : group * routes + k + 1, :] for k in range(routes))
            parts.append(jnp.sum(hot * weight, axis=1, keepdims=True))
        outs[m][:, 2 * width :] = jnp.where(lane == 0, parts[0], jnp.where(lane == 1, parts[1], 0.0)).astype(BF16)


def stacked(refs, low, high):
    return jnp.concatenate([r[:, low:high].astype(F32) for r in refs], axis=0)


def expert_kernel(routes, slots, rank, *refs):
    rows_in = refs[:PLANE]
    gate_w, up_w, down_w, gate_a, gate_b, up_a, up_b, down_a, down_b = refs[PLANE : PLANE + 9]
    outs = refs[PLANE + 9 : 2 * PLANE + 9]
    acts_ref, lows_ref = refs[2 * PLANE + 9 :]
    width, hidden_units = gate_w.shape
    x = stacked(rows_in, 0, width).astype(BF16)
    g = stacked(rows_in, width, 2 * width).astype(BF16)
    side = stacked(rows_in, 2 * width, 2 * width + LANES)
    weight = side[:, 0:1] + side[:, 1:2]

    low_gate = nt(x, gate_a[...]).astype(BF16)
    low_up = nt(x, up_a[...]).astype(BF16)
    gate_pre = nn(x, gate_w[...]) + SCALE * nn(low_gate, gate_b[...])
    up_pre = nn(x, up_w[...]) + SCALE * nn(low_up, up_b[...])
    q = jax.nn.sigmoid(gate_pre)
    silu = gate_pre * q
    hidden = (silu * up_pre).astype(BF16)
    low_down = nt(hidden, down_a[...]).astype(BF16)
    g_hidden = nt(g, down_w[...])
    g_low = nt(g, down_b[...])
    dots = jnp.sum(hidden.astype(F32) * g_hidden, axis=1, keepdims=True) + SCALE * jnp.sum(
        low_down.astype(F32) * g_low, axis=1, keepdims=True
    )
    down_back = (weight * g_low).astype(BF16)
    weighted_low = (weight * low_down.astype(F32)).astype(BF16)
    grad_hidden = weight * g_hidden + SCALE * nn(down_back, down_a[...])
    gate_grad = (grad_hidden * up_pre * q * (1.0 + gate_pre * (1.0 - q))).astype(BF16)
    up_grad = (grad_hidden * silu).astype(BF16)
    gate_back = nt(gate_grad, gate_b[...]).astype(BF16)
    up_back = nt(up_grad, up_b[...]).astype(BF16)
    input_grad = (
        nt(gate_grad, gate_w[...])
        + nt(up_grad, up_w[...])
        + SCALE * (nn(gate_back, gate_a[...]) + nn(up_back, up_a[...]))
    )
    high, low = two_parts(dots)
    lane = lax.broadcasted_iota(jnp.int32, (PLANE * slots, LANES), 1)
    side_back = jnp.where(lane < routes, high, jnp.where(lane < 2 * routes, low, 0.0))
    for m in range(PLANE):
        rows = slice(m * slots, (m + 1) * slots)
        outs[m][:, :width] = input_grad[rows].astype(BF16)
        outs[m][:, width:] = side_back[rows].astype(BF16)
    acts_ref[:, :hidden_units] = hidden
    acts_ref[:, hidden_units : 2 * hidden_units] = gate_grad
    acts_ref[:, 2 * hidden_units :] = up_grad
    for i, value in enumerate((gate_back, low_gate, up_back, low_up, down_back, weighted_low)):
        lows_ref[:, i * rank : (i + 1) * rank] = value.astype(F32)
    lows_ref[:, 6 * rank :] = jnp.zeros((PLANE * slots, lows_ref.shape[1] - 6 * rank), F32)


def combine_kernel(routes, slots, info_ref, side_ref, *refs):
    backs, out_ref = refs[:PLANE], refs[PLANE]
    width = backs[0].shape[1] - LANES
    side = side_ref[...].astype(F32)
    names = [info_ref[m].astype(F32) + 1.0 for m in range(PLANE)]
    _, found = one_hots(names, slots, side, routes)
    turned = [hot.T.astype(BF16) for hot, _ in found]
    total = jnp.zeros((side.shape[0], LANES), F32)
    for m in range(PLANE):
        total = total + jnp.where(side == names[m], nn(turned[m], backs[m][:, width:]), 0.0)
    out_ref[:, width:] = total.astype(BF16)
    rows = stacked(backs, 0, width).astype(BF16)
    picks = jnp.concatenate([hot for hot, _ in found], axis=0)
    out_ref[:, :width] = lax.dot_general(
        picks.astype(BF16), rows, (((0,), (0,)), ((), ())), preferred_element_type=F32
    ).astype(BF16)


def finish_kernel(routes, *refs):
    parts, (tokens_ref, combine_ref) = refs[:-2], refs[-2:]
    width = tokens_ref.shape[1]
    tokens_ref[...] = sum(r[:, :width].astype(F32) for r in parts).astype(BF16)
    side = sum(r[:, width:].astype(F32) for r in parts)
    combine_ref[...] = side[:, :routes] + side[:, routes : 2 * routes]


def adapter_kernel(stages, rank, *refs):
    rows_in = refs[: stages * PLANE]
    acts = refs[stages * PLANE : stages * (PLANE + 1)]
    lows = refs[stages * (PLANE + 1) : stages * (PLANE + 2)]
    gate_in, gate_out, up_in, up_out, down_in, down_out = refs[stages * (PLANE + 2) :]
    width, hidden_units = gate_in.shape[2], gate_out.shape[2]
    turned = jnp.concatenate([r[...] for r in lows], axis=0).T.astype(BF16)
    part = [turned[i * rank : (i + 1) * rank] for i in range(6)]
    x = stacked(rows_in, 0, width).astype(BF16)
    g = stacked(rows_in, width, 2 * width).astype(BF16)
    hidden = jnp.concatenate([r[:, :hidden_units] for r in acts], axis=0)
    gate_grad = jnp.concatenate([r[:, hidden_units : 2 * hidden_units] for r in acts], axis=0)
    up_grad = jnp.concatenate([r[:, 2 * hidden_units :] for r in acts], axis=0)
    gate_in[0] = SCALE * nn(part[0], x)
    gate_out[0] = SCALE * nn(part[1], gate_grad)
    up_in[0] = SCALE * nn(part[2], x)
    up_out[0] = SCALE * nn(part[3], up_grad)
    down_in[0] = SCALE * nn(part[4], hidden)
    down_out[0] = SCALE * nn(part[5], g)


def on_device(tokens, grad_out, expert_ids, combine, *weights):
    rows, width = tokens.shape
    routes = expert_ids.shape[1]
    experts = lax.axis_size("expert")
    planes = experts // PLANE
    capacity = rows * routes * 9 // (8 * experts)
    slots = -(-capacity // 8) * 8
    matrices = [w[0] for w in weights]
    hidden_units = matrices[0].shape[1]
    rank = matrices[3].shape[0]
    low_lanes = -(-6 * rank // LANES) * LANES
    wide = width + LANES
    shape = jax.ShapeDtypeStruct

    me = lax.axis_index("expert").astype(jnp.int32)
    here, seat = me // PLANE, me % PLANE
    names = jnp.stack([here * PLANE + (seat ^ m) for m in range(PLANE)])

    def along(value, step):
        pairs = [
            (p * PLANE + s, (p + step) * PLANE + s) for p in range(planes) for s in range(PLANE) if 0 <= p + step < planes
        ]
        return lax.ppermute(value, "expert", pairs)

    def flipped(value, mask):
        return lax.ppermute(value, "expert", [(i, i ^ mask) for i in range(experts)])

    packed = pl.pallas_call(
        functools.partial(pack_kernel, routes),
        out_shape=shape((rows, wide), BF16),
        in_specs=[vmem()] * 3,
        out_specs=vmem(),
        compiler_params=params(),
        cost_estimate=cost(0, 4 * rows * width),
        name="pack",
    )(grad_out, expert_ids, combine)

    blocks = {0: (tokens, packed)}
    for step in range(1, planes):
        for sign in (1, -1):
            x, g = blocks[sign * (step - 1)]
            blocks[sign * step] = (along(x, -sign), along(g, -sign))

    def select(stage):
        offsets = sorted({(p ^ stage) - p for p in range(planes)}, key=lambda o: (abs(o), o))
        mine = (here ^ stage) - here
        choice = sum(jnp.where(mine == o, i, 0) for i, o in enumerate(offsets))
        info = jnp.concatenate([names, jnp.reshape(choice, (1,))]).astype(jnp.int32)
        choices = len(offsets)
        return pl.pallas_call(
            functools.partial(select_kernel, routes, slots, choices),
            out_shape=[shape((slots, 2 * width + LANES), BF16)] * PLANE + [shape((rows, LANES), BF16)],
            in_specs=[smem()] + [anywhere()] * (2 * choices),
            out_specs=[vmem()] * (PLANE + 1),
            scratch_shapes=[
                pltpu.VMEM((rows, width), BF16),
                pltpu.VMEM((rows, wide), BF16),
                pltpu.SemaphoreType.DMA,
                pltpu.SemaphoreType.DMA,
            ],
            compiler_params=params(),
            cost_estimate=cost(4 * PLANE * slots * rows * width, 4 * rows * width + 4 * PLANE * slots * width),
            name="select",
        )(info, *[blocks[o][0] for o in offsets], *[blocks[o][1] for o in offsets])

    def expert(got):
        return pl.pallas_call(
            functools.partial(expert_kernel, routes, slots, rank),
            out_shape=[shape((slots, wide), BF16)] * PLANE
            + [shape((PLANE * slots, 3 * hidden_units), BF16), shape((PLANE * slots, low_lanes), F32)],
            in_specs=[vmem()] * (PLANE + 9),
            out_specs=[vmem()] * (PLANE + 2),
            compiler_params=params(),
            cost_estimate=cost(
                10 * PLANE * slots * width * hidden_units, 6 * width * hidden_units, PLANE * slots * hidden_units
            ),
            name="expert",
        )(*got, *matrices)

    def gather_back(side, backs):
        return pl.pallas_call(
            functools.partial(combine_kernel, routes, slots),
            out_shape=shape((rows, wide), BF16),
            in_specs=[smem()] + [vmem()] * (PLANE + 1),
            out_specs=vmem(),
            compiler_params=params(),
            cost_estimate=cost(2 * PLANE * slots * rows * width, 2 * (rows + PLANE * slots) * width),
            name="combine",
        )(names, side, *backs)

    parts, received, acts, lows = [], [], [], []
    for stage in range(planes):
        *picked, side = select(stage)
        got = [picked[0]] + [flipped(picked[m], m) for m in range(1, PLANE)]
        *backs, act, low = expert(got)
        returned = [backs[0]] + [flipped(backs[m], m) for m in range(1, PLANE)]
        part = gather_back(side, returned)
        parts.append(part if stage == 0 else flipped(part, stage * PLANE))
        received += got
        acts.append(act)
        lows.append(low)

    grad_tokens, grad_combine = pl.pallas_call(
        functools.partial(finish_kernel, routes),
        out_shape=[shape((rows, width), BF16), shape((rows, routes), F32)],
        in_specs=[vmem()] * planes,
        out_specs=[vmem()] * 2,
        compiler_params=params(),
        cost_estimate=cost(0, 2 * (planes + 1) * rows * width),
        name="finish",
    )(*parts)
    sides = [width, hidden_units, width, hidden_units, hidden_units, width]
    total = planes * PLANE * slots
    grads = pl.pallas_call(
        functools.partial(adapter_kernel, planes, rank),
        out_shape=[shape((1, rank, s), F32) for s in sides],
        in_specs=[vmem()] * (planes * (PLANE + 2)),
        out_specs=[vmem()] * 6,
        compiler_params=params(),
        cost_estimate=cost(2 * rank * total * sum(sides), total * (4 * width + 6 * hidden_units)),
        name="adapter_grads",
    )(*received, *acts, *lows)
    return (grad_tokens, grad_combine, *grads)


def solution(mesh):
    by_token = P(("groups", "expert"), None)
    by_part = P(("groups", "expert"), None, None)
    return jax.shard_map(
        on_device,
        mesh=mesh,
        in_specs=(by_token,) * 4 + (P("expert", None, None),) * 9,
        out_specs=(by_token,) * 2 + (by_part,) * 6,
        check_vma=False,
    )
```

```python
import functools

import jax
import jax.numpy as jnp
from jax import lax
from jax.experimental import pallas as pl
from jax.experimental.pallas import tpu as pltpu
from jax.sharding import PartitionSpec as P

SCALE = 2.0
PLANE = 4
LANES = 128
F32 = jnp.float32
BF16 = jnp.bfloat16
MIB = 1024 * 1024
RATE = 3000000


def nn(a, b):
    return lax.dot_general(a, b, (((1,), (0,)), ((), ())), preferred_element_type=F32)


def nt(a, b):
    return lax.dot_general(a, b, (((1,), (1,)), ((), ())), preferred_element_type=F32)


def two_parts(value):
    high = value.astype(BF16).astype(F32)
    return high, value - high


def smem():
    return pl.BlockSpec(memory_space=pltpu.SMEM)


def one_hots(names, slots, side, routes):
    turned = side.T
    tokens = side.shape[0]
    earlier = lax.broadcasted_iota(jnp.int32, (tokens, tokens), 0)
    later = lax.broadcasted_iota(jnp.int32, (tokens, tokens), 1)
    ahead = jnp.where(earlier < later, 1.0, 0.0).astype(BF16)
    place = lax.broadcasted_iota(jnp.int32, (slots, tokens), 0).astype(F32)
    found = []
    for name in names:
        hits = [jnp.where(turned[k : k + 1, :] == name, 1.0, 0.0) for k in range(routes)]
        member = sum(hits)
        wide = jnp.broadcast_to(member, (8, tokens)).astype(BF16)
        slot = nn(wide, ahead)[0:1, :]
        found.append((jnp.where((place == slot) & (member > 0.0), 1.0, 0.0), hits))
    return turned, found


def pack_kernel(routes, x_ref, grad_ref, ids_ref, weight_ref, out_ref):
    tokens, width = grad_ref.shape
    out_ref[:, :width] = x_ref[...]
    out_ref[:, width : 2 * width] = grad_ref[...]
    names = ids_ref[...].astype(F32) + 1.0
    high, low = two_parts(weight_ref[...])
    row = lax.broadcasted_iota(jnp.int32, (LANES, tokens), 0)
    side = jnp.zeros((LANES, tokens), F32)
    for group, values in enumerate((names, names, high, low)):
        for k in range(routes):
            side = jnp.where(row == group * routes + k, values[k : k + 1, :], side)
    out_ref[:, 2 * width :] = side.T.astype(BF16)


def select_kernel(routes, slots, choices, stage, info_ref, *refs):
    blocks, outs, side_ref = refs[:choices], refs[choices:-1], refs[-1]
    block = blocks[0]
    for i in range(1, choices):

        @pl.when(info_ref[PLANE + stage] == i)
        def _():
            block[...] = blocks[i][...]

    width = (block.shape[1] - LANES) // 2
    side_ref[...] = block[:, 2 * width :]
    side = block[:, 2 * width :].astype(F32)
    names = [info_ref[m].astype(F32) + 1.0 for m in range(PLANE)]
    turned, found = one_hots(names, slots, side, routes)
    lane = lax.broadcasted_iota(jnp.int32, (slots, LANES), 1)
    picks = jnp.concatenate([hot for hot, _ in found], axis=0).astype(BF16)
    chosen = nn(picks, block[:, : 2 * width])
    tails = []
    for hot, hits in found:
        parts = []
        for group in (2, 3):
            weight = sum(hits[k] * turned[group * routes + k : group * routes + k + 1, :] for k in range(routes))
            parts.append(jnp.sum(hot * weight, axis=1, keepdims=True))
        tails.append(jnp.where(lane == 0, parts[0], jnp.where(lane == 1, parts[1], 0.0)))
    for out, low, high in ((outs[0], 0, 1), (outs[1], 1, 2), (outs[2], 2, 4)):
        out[:, : 2 * width] = chosen[low * slots : high * slots].astype(BF16)
        out[:, 2 * width :] = jnp.concatenate(tails[low:high], axis=0).astype(BF16)


def stacked(refs, low, high):
    own, near, across, around = (r[:, low:high].astype(F32) for r in refs)
    half = own.shape[0]
    return jnp.concatenate([own, near, across[:half], around[half:]], axis=0)


def prepare_kernel(gate_a, gate_b, up_a, up_b, down_a, down_b, *refs):
    def padded(*parts):
        rows, columns = sum(p.shape[0] for p in parts), parts[0].shape[1]
        return jnp.concatenate([*(p.astype(F32) for p in parts), jnp.zeros((LANES - rows, columns), F32)], axis=0)

    in_t, in_s, back_t, out_s, down_t, down_s, last_t = refs
    rank = gate_a.shape[0]
    both = padded(gate_a[...], up_a[...])
    in_t[...] = both.T.astype(BF16)
    in_s[...] = both.astype(BF16)
    gate = padded(gate_b[...])
    up = padded(jnp.zeros((rank, up_b.shape[1]), F32), up_b[...])
    out_s[0] = gate.astype(BF16)
    out_s[1] = up.astype(BF16)
    back_t[0] = gate.T.astype(BF16)
    back_t[1] = up.T.astype(BF16)
    down = padded(down_a[...])
    down_s[...] = down.astype(BF16)
    down_t[...] = down.T.astype(BF16)
    last_t[...] = padded(down_b[...]).T.astype(BF16)


def expert_kernel(routes, slots, *refs):
    rows_in = refs[:PLANE]
    in_t, in_s, back_t, out_s, down_t, down_s, last_t, gate_w, up_w, down_w = refs[PLANE : PLANE + 10]
    *outs, acts_ref, lows_ref = refs[PLANE + 10 :]
    width, hidden_units = gate_w.shape
    x = stacked(rows_in, 0, width).astype(BF16)
    g = stacked(rows_in, width, 2 * width).astype(BF16)
    side = stacked(rows_in, 2 * width, 2 * width + LANES)
    weight = side[:, 0:1] + side[:, 1:2]

    low = nn(x, in_t[...]).astype(BF16)
    g_low = nn(g, last_t[...])
    down_back = (weight * g_low).astype(BF16)
    gate_pre = nn(x, gate_w[...]) + SCALE * nn(low, out_s[0])
    up_pre = nn(x, up_w[...]) + SCALE * nn(low, out_s[1])
    q = jax.nn.sigmoid(gate_pre)
    silu = gate_pre * q
    hidden = (silu * up_pre).astype(BF16)
    low_down = nn(hidden, down_t[...]).astype(BF16).astype(F32)
    g_hidden = nt(g, down_w[...])
    dots = jnp.sum(hidden.astype(F32) * g_hidden, axis=1, keepdims=True)
    dots = dots + SCALE * jnp.sum(low_down * g_low, axis=1, keepdims=True)
    grad_hidden = weight * g_hidden + SCALE * nn(down_back, down_s[...])
    gate_grad = (grad_hidden * up_pre * q * (1.0 + gate_pre * (1.0 - q))).astype(BF16)
    up_grad = (grad_hidden * silu).astype(BF16)
    back = (nn(gate_grad, back_t[0]) + nn(up_grad, back_t[1])).astype(BF16)
    input_grad = nt(gate_grad, gate_w[...]) + nt(up_grad, up_w[...]) + SCALE * nn(back, in_s[...])
    high, lesser = two_parts(dots)
    lane = lax.broadcasted_iota(jnp.int32, (PLANE * slots, LANES), 1)
    side_back = jnp.where(lane < routes, high, jnp.where(lane < 2 * routes, lesser, 0.0))
    for out, first, end in ((outs[0], 0, 1), (outs[1], 1, 2), (outs[2], 2, 4)):
        out[:, :width] = input_grad[first * slots : end * slots].astype(BF16)
        out[:, width:] = side_back[first * slots : end * slots].astype(BF16)
    acts_ref[:, :hidden_units] = hidden
    acts_ref[:, hidden_units : 2 * hidden_units] = gate_grad
    acts_ref[:, 2 * hidden_units :] = up_grad
    for n, value in enumerate((back, low, down_back, (weight * low_down).astype(BF16))):
        lows_ref[:, n * LANES : (n + 1) * LANES] = value


def combine_kernel(routes, slots, info_ref, side_ref, *refs):
    backs, out_ref = refs[:PLANE], refs[PLANE]
    width = out_ref.shape[1] - LANES
    side = side_ref[...].astype(F32)
    names = [info_ref[m].astype(F32) + 1.0 for m in range(PLANE)]
    _, found = one_hots(names, slots, side, routes)
    tails = stacked(backs, width, width + LANES).astype(BF16)
    extra = jnp.zeros((side.shape[0], LANES), F32)
    for m in range(PLANE):
        hot = jnp.concatenate([h if n == m else jnp.zeros_like(h) for n, (h, _) in enumerate(found)], axis=0)
        spread = lax.dot_general(hot.astype(BF16), tails, (((0,), (0,)), ((), ())), preferred_element_type=F32)
        extra = extra + jnp.where(side == names[m], spread, 0.0)
    out_ref[:, width:] = extra.astype(BF16)
    picks = jnp.concatenate([hot for hot, _ in found], axis=0).astype(BF16)
    rows = stacked(backs, 0, width).astype(BF16)
    out_ref[:, :width] = lax.dot_general(
        picks, rows, (((0,), (0,)), ((), ())), preferred_element_type=F32
    ).astype(BF16)


def add_kernel(*refs):
    refs[-1][...] = sum(r[...].astype(F32) for r in refs[:-1])


def finish_kernel(routes, *refs):
    parts, (tokens_ref, combine_ref) = refs[:-2], refs[-2:]
    width = tokens_ref.shape[1]
    tokens_ref[...] = sum(r[:, :width].astype(F32) for r in parts).astype(BF16)
    side = sum(r[:, width:].astype(F32) for r in parts).T
    combine_ref[...] = side[:routes] + side[routes : 2 * routes]


def adapter_kernel(stages, rank, *refs):
    rows_in, refs = refs[: stages * PLANE], refs[stages * PLANE :]
    acts, lows, outs = refs[:stages], refs[stages : 2 * stages], refs[2 * stages :]
    width, hidden_units = outs[0].shape[2], outs[1].shape[2]

    def over_rows(part, other):
        return SCALE * lax.dot_general(part, other, (((0,), (0,)), ((), ())), preferred_element_type=F32)

    def every(low, high):
        pieces = [stacked(rows_in[n * PLANE : (n + 1) * PLANE], low, high) for n in range(stages)]
        return jnp.concatenate(pieces, axis=0).astype(BF16)

    parts = [jnp.concatenate([r[:, n * LANES : (n + 1) * LANES] for r in lows], axis=0) for n in range(4)]
    act = [jnp.concatenate([r[:, n * hidden_units : (n + 1) * hidden_units] for r in acts], axis=0) for n in range(3)]
    by_x = over_rows(parts[0], every(0, width))
    outs[0][0] = by_x[:rank]
    outs[2][0] = by_x[rank : 2 * rank]
    outs[1][0] = over_rows(parts[1], act[1])[:rank]
    outs[3][0] = over_rows(parts[1], act[2])[rank : 2 * rank]
    outs[4][0] = over_rows(parts[2], act[0])[:rank]
    outs[5][0] = over_rows(parts[3], every(width, 2 * width))[:rank]


def on_device(tokens, grad_out, expert_ids, combine, *weights):
    rows, width = tokens.shape
    routes = expert_ids.shape[1]
    experts = lax.axis_size("expert")
    planes = experts // PLANE
    capacity = rows * routes * 9 // (8 * experts)
    slots = -(-capacity // 8) * 8
    matrices = [w[0] for w in weights]
    hidden_units = matrices[0].shape[1]
    rank = matrices[3].shape[0]
    wide = width + LANES
    shape = jax.ShapeDtypeStruct

    me = lax.axis_index("expert").astype(jnp.int32)
    here, seat = me // PLANE, me % PLANE
    if planes == 4:
        end = ((here == 0) | (here == 3)).astype(jnp.int32)
        choice = [0 * end, 0 * end, end, end]
    else:
        offsets = [sorted({(p ^ n) - p for p in range(planes)}, key=lambda o: (abs(o), o)) for n in range(planes)]
        choice = [sum(jnp.where((here ^ n) - here == o, i, 0) for i, o in enumerate(offsets[n])) for n in range(planes)]
    info = jnp.stack([here * PLANE + (seat ^ m) for m in range(PLANE)] + choice).astype(jnp.int32)

    def along(value, step):
        pairs = [
            (p * PLANE + s, (p + step) * PLANE + s) for p in range(planes) for s in range(PLANE) if 0 <= p + step < planes
        ]
        return lax.ppermute(value, "expert", pairs)

    def flipped(value, mask, sources=range(planes)):
        pairs = [(p * PLANE + n, (p * PLANE + n) ^ mask) for p in sources for n in range(PLANE)]
        return lax.ppermute(value, "expert", pairs)

    def kernel(body, outs, args, micros, name, mib, scalars=0):
        vmem = pl.BlockSpec(memory_space=pltpu.VMEM)

        def run(*refs):
            refs[len(args) + len(last) + len(outs)][...] = jnp.zeros((8, LANES), F32)
            body(*refs[: len(args)], *refs[len(args) + len(last) : -1])

        *result, mark = pl.pallas_call(
            run,
            out_shape=[*outs, shape((8, LANES), F32)],
            in_specs=[smem()] * scalars + [vmem] * (len(args) - scalars + len(last)),
            out_specs=[vmem] * (len(outs) + 1),
            compiler_params=pltpu.CompilerParams(vmem_limit_bytes=mib * MIB),
            cost_estimate=pl.CostEstimate(flops=1, bytes_accessed=micros * RATE, transcendentals=0),
            name=name,
        )(*args, *last)
        last[:] = [mark]
        return result

    last = []
    (packed,) = kernel(
        functools.partial(pack_kernel, routes),
        [shape((rows, 2 * width + LANES), BF16)],
        (tokens, grad_out, expert_ids.T, combine.T),
        2,
        "pack",
        6,
    )

    def expert(got):
        return kernel(
            functools.partial(expert_kernel, routes, slots),
            [shape((n * slots, wide), BF16) for n in (1, 1, 2)]
            + [shape((PLANE * slots, 3 * hidden_units), BF16), shape((PLANE * slots, 4 * LANES), BF16)],
            (*got, *adapters, *matrices[:3]),
            8,
            "expert",
            20,
        )

    def together(*values):
        *values, last[0] = lax.optimization_barrier((*values, last[0]))
        return values

    rows_of, sides, parts, acts, lows = {}, {}, {}, {}, {}

    def halfway(own, near, far, sources):
        return own, flipped(near, 1), flipped(far, 2, sources)

    def arrived(own, near, across):
        (across,) = together(across)
        return own, near, across, flipped(across, 1)

    def begin(stage, *found, sources=range(planes)):
        *picked, sides[stage] = kernel(
            functools.partial(select_kernel, routes, slots, len(found), stage),
            [shape((n * slots, 2 * width + LANES), BF16) for n in (1, 1, 2)] + [shape((rows, LANES), BF16)],
            (info, *found),
            4,
            "select",
            12,
            scalars=1,
        )
        rows_of[stage] = halfway(*picked, sources)

    def middle_of(stage, sources=range(planes)):
        rows_of[stage] = arrived(*rows_of[stage])
        *backs, acts[stage], lows[stage] = expert(rows_of[stage])
        parts[stage] = halfway(*backs, sources)

    def end_of(stage, toward, sources=range(planes)):
        (part,) = kernel(
            functools.partial(combine_kernel, routes, slots),
            [shape((rows, wide), BF16)],
            (info, sides[stage], *arrived(*parts[stage])),
            3,
            "combine",
            8,
            scalars=1,
        )
        parts[stage] = flipped(part, toward * PLANE, sources) if toward else part

    def add(*values):
        return kernel(add_kernel, [shape((rows, wide), F32)], values, 1, "add", 8)[0]

    adapters = []

    def prepare():
        adapters[:] = kernel(
            prepare_kernel,
            [
                shape((width, LANES), BF16),
                shape((LANES, width), BF16),
                shape((2, hidden_units, LANES), BF16),
                shape((2, LANES, hidden_units), BF16),
                shape((hidden_units, LANES), BF16),
                shape((LANES, hidden_units), BF16),
                shape((width, LANES), BF16),
            ],
            tuple(matrices[3:]),
            4,
            "prepare",
            8,
        )

    if planes == 4:
        mids = (1, 2)
        mate, across = flipped(packed, PLANE), flipped(packed, 3 * PLANE, mids)
        begin(0, packed)
        prepare()
        mate, across = together(mate, across)
        mate_across, far = flipped(mate, 3 * PLANE, mids), flipped(across, PLANE)
        begin(1, mate)
        middle_of(0)
        mate_across, far, *rows_of[1] = together(mate_across, far, *rows_of[1])
        farthest = flipped(mate_across, PLANE)
        begin(2, mate_across, far)
        middle_of(1)
        middle_of(2)
        (farthest,) = together(farthest)
        begin(3, across, farthest)
        end_of(2, 2)
        middle_of(3)
        end_of(1, 1)
        (parts[2],) = together(parts[2])
        end_of(3, 3)
        end_of(0, 0)
    else:
        blocks = {0: packed}
        for step in range(1, planes):
            for sign in (1, -1):
                blocks[sign * step] = along(blocks[sign * (step - 1)], -sign)
        prepare()
        for stage in range(planes):
            begin(stage, *(blocks[o] for o in offsets[stage]))
            middle_of(stage)
            end_of(stage, stage)
    order = sorted(rows_of)
    total = add(*(parts[n] for n in order[:-1]))

    grads = kernel(
        functools.partial(adapter_kernel, len(order), rank),
        [shape((1, rank, n), F32) for n in (width, hidden_units, width, hidden_units, hidden_units, width)],
        (*(r for n in order for r in rows_of[n]), *(acts[n] for n in order), *(lows[n] for n in order)),
        5,
        "adapter_grads",
        24,
    )
    grad_tokens, grad_combine = kernel(
        functools.partial(finish_kernel, routes),
        [shape((rows, width), BF16), shape((routes, rows), F32)],
        (total, parts[order[-1]]),
        3,
        "finish",
        8,
    )
    return (grad_tokens, grad_combine.T, *grads)


def solution(mesh):
    by_token = P(("groups", "expert"), None)
    by_part = P(("groups", "expert"), None, None)
    return jax.shard_map(
        on_device,
        mesh=mesh,
        in_specs=(by_token,) * 4 + (P("expert", None, None),) * 9,
        out_specs=(by_token,) * 2 + (by_part,) * 6,
        check_vma=False,
    )
```

```python
import functools

import jax
import jax.numpy as jnp
from jax import lax
from jax.experimental import pallas as pl
from jax.experimental.pallas import tpu as pltpu
from jax.sharding import PartitionSpec as P

SCALE = 2.0
PLANE = 4
LANES = 128
F32 = jnp.float32
BF16 = jnp.bfloat16
MIB = 1024 * 1024
RATE = 3000000


def nn(a, b):
    return lax.dot_general(a, b, (((1,), (0,)), ((), ())), preferred_element_type=F32)


def nt(a, b):
    return lax.dot_general(a, b, (((1,), (1,)), ((), ())), preferred_element_type=F32)


def two_parts(value):
    high = value.astype(BF16).astype(F32)
    return high, value - high


def smem():
    return pl.BlockSpec(memory_space=pltpu.SMEM)


def one_hots(names, slots, side, routes):
    turned = side.T
    tokens = side.shape[0]
    earlier = lax.broadcasted_iota(jnp.int32, (tokens, tokens), 0)
    later = lax.broadcasted_iota(jnp.int32, (tokens, tokens), 1)
    ahead = jnp.where(earlier < later, 1.0, 0.0).astype(BF16)
    place = lax.broadcasted_iota(jnp.int32, (slots, tokens), 0).astype(F32)
    found = []
    for name in names:
        hits = [jnp.where(turned[k : k + 1, :] == name, 1.0, 0.0) for k in range(routes)]
        member = sum(hits)
        wide = jnp.broadcast_to(member, (8, tokens)).astype(BF16)
        slot = nn(wide, ahead)[0:1, :]
        found.append((jnp.where((place == slot) & (member > 0.0), 1.0, 0.0), hits))
    return turned, found


def pack_kernel(routes, x_ref, grad_ref, ids_ref, weight_ref, out_ref, ids_buf, weight_buf, sems):
    tokens, width = grad_ref.shape
    targets = (out_ref.at[:, :width], out_ref.at[:, width : 2 * width], ids_buf, weight_buf)
    sources = (x_ref, grad_ref, ids_ref, weight_ref)
    copies = [pltpu.make_async_copy(a, b, sems.at[n]) for n, (a, b) in enumerate(zip(sources, targets))]
    for copy in copies:
        copy.start()
    copies[2].wait()
    copies[3].wait()
    names = ids_buf[...].astype(F32) + 1.0
    high, low = two_parts(weight_buf[...])
    row = lax.broadcasted_iota(jnp.int32, (LANES, tokens), 0)
    side = jnp.zeros((LANES, tokens), F32)
    for group, values in enumerate((names, names, high, low)):
        for k in range(routes):
            side = jnp.where(row == group * routes + k, values[k : k + 1, :], side)
    out_ref[:, 2 * width :] = side.T.astype(BF16)
    copies[0].wait()
    copies[1].wait()


def select_kernel(routes, slots, choices, stage, info_ref, *refs):
    blocks, outs, side_ref = refs[:choices], refs[choices:-1], refs[-1]
    block = blocks[0]
    for i in range(1, choices):

        @pl.when(info_ref[PLANE + stage] == i)
        def _():
            block[...] = blocks[i][...]

    width = (block.shape[1] - LANES) // 2
    side_ref[...] = block[:, 2 * width :]
    side = block[:, 2 * width :].astype(F32)
    names = [info_ref[m].astype(F32) + 1.0 for m in range(PLANE)]
    turned, found = one_hots(names, slots, side, routes)
    lane = lax.broadcasted_iota(jnp.int32, (slots, LANES), 1)
    picks = jnp.concatenate([hot for hot, _ in found], axis=0).astype(BF16)
    chosen = nn(picks, block[:, : 2 * width])
    tails = []
    for hot, hits in found:
        parts = []
        for group in (2, 3):
            weight = sum(hits[k] * turned[group * routes + k : group * routes + k + 1, :] for k in range(routes))
            parts.append(jnp.sum(hot * weight, axis=1, keepdims=True))
        tails.append(jnp.where(lane == 0, parts[0], jnp.where(lane == 1, parts[1], 0.0)))
    for out, low, high in ((outs[0], 0, 1), (outs[1], 1, 2), (outs[2], 2, 4)):
        out[:, : 2 * width] = chosen[low * slots : high * slots].astype(BF16)
        out[:, 2 * width :] = jnp.concatenate(tails[low:high], axis=0).astype(BF16)


def stacked(refs, low, high):
    own, near, across, around = (r[:, low:high].astype(F32) for r in refs)
    half = own.shape[0]
    return jnp.concatenate([own, near, across[:half], around[half:]], axis=0)


def prepare_kernel(gate_a, gate_b, up_a, up_b, down_a, down_b, *refs):
    def padded(*parts):
        rows, columns = sum(p.shape[0] for p in parts), parts[0].shape[1]
        return jnp.concatenate([*(p.astype(F32) for p in parts), jnp.zeros((LANES - rows, columns), F32)], axis=0)

    in_t, in_s, back_t, out_s, down_t, down_s, last_t = refs
    rank = gate_a.shape[0]
    both = padded(gate_a[...], up_a[...])
    in_t[...] = both.T.astype(BF16)
    in_s[...] = both.astype(BF16)
    gate = padded(gate_b[...])
    up = padded(jnp.zeros((rank, up_b.shape[1]), F32), up_b[...])
    out_s[0] = gate.astype(BF16)
    out_s[1] = up.astype(BF16)
    back_t[0] = gate.T.astype(BF16)
    back_t[1] = up.T.astype(BF16)
    down = padded(down_a[...])
    down_s[...] = down.astype(BF16)
    down_t[...] = down.T.astype(BF16)
    last_t[...] = padded(down_b[...]).T.astype(BF16)


def expert_kernel(routes, slots, *refs):
    rows_in = refs[:PLANE]
    in_t, in_s, back_t, out_s, down_t, down_s, last_t, gate_w, up_w, down_w = refs[PLANE : PLANE + 10]
    *outs, acts_ref, lows_ref = refs[PLANE + 10 :]
    width, hidden_units = gate_w.shape
    x = stacked(rows_in, 0, width).astype(BF16)
    g = stacked(rows_in, width, 2 * width).astype(BF16)
    side = stacked(rows_in, 2 * width, 2 * width + LANES)
    weight = side[:, 0:1] + side[:, 1:2]

    low = nn(x, in_t[...]).astype(BF16)
    g_low = nn(g, last_t[...])
    down_back = (weight * g_low).astype(BF16)
    gate_pre = nn(x, gate_w[...]) + SCALE * nn(low, out_s[0])
    up_pre = nn(x, up_w[...]) + SCALE * nn(low, out_s[1])
    q = jax.nn.sigmoid(gate_pre)
    silu = gate_pre * q
    hidden = (silu * up_pre).astype(BF16)
    low_down = nn(hidden, down_t[...]).astype(BF16).astype(F32)
    g_hidden = nt(g, down_w[...])
    dots = jnp.sum(hidden.astype(F32) * g_hidden, axis=1, keepdims=True)
    dots = dots + SCALE * jnp.sum(low_down * g_low, axis=1, keepdims=True)
    grad_hidden = weight * g_hidden + SCALE * nn(down_back, down_s[...])
    gate_grad = (grad_hidden * up_pre * q * (1.0 + gate_pre * (1.0 - q))).astype(BF16)
    up_grad = (grad_hidden * silu).astype(BF16)
    back = (nn(gate_grad, back_t[0]) + nn(up_grad, back_t[1])).astype(BF16)
    input_grad = nt(gate_grad, gate_w[...]) + nt(up_grad, up_w[...]) + SCALE * nn(back, in_s[...])
    high, lesser = two_parts(dots)
    lane = lax.broadcasted_iota(jnp.int32, (PLANE * slots, LANES), 1)
    side_back = jnp.where(lane < routes, high, jnp.where(lane < 2 * routes, lesser, 0.0))
    for out, first, end in ((outs[0], 0, 1), (outs[1], 1, 2), (outs[2], 2, 4)):
        out[:, :width] = input_grad[first * slots : end * slots].astype(BF16)
        out[:, width:] = side_back[first * slots : end * slots].astype(BF16)
    acts_ref[:, :hidden_units] = hidden
    acts_ref[:, hidden_units : 2 * hidden_units] = gate_grad
    acts_ref[:, 2 * hidden_units :] = up_grad
    for n, value in enumerate((back, low, down_back, (weight * low_down).astype(BF16))):
        lows_ref[:, n * LANES : (n + 1) * LANES] = value


def combine_kernel(routes, slots, info_ref, side_ref, *refs):
    backs, outs = refs[:PLANE], refs[PLANE:]
    width = backs[0].shape[1] - LANES
    side = side_ref[...].astype(F32)
    names = [info_ref[m].astype(F32) + 1.0 for m in range(PLANE)]
    _, found = one_hots(names, slots, side, routes)
    tails = stacked(backs, width, width + LANES).astype(BF16)
    extra = jnp.zeros((side.shape[0], LANES), F32)
    for m in range(PLANE):
        hot = jnp.concatenate([h if n == m else jnp.zeros_like(h) for n, (h, _) in enumerate(found)], axis=0)
        spread = lax.dot_general(hot.astype(BF16), tails, (((0,), (0,)), ((), ())), preferred_element_type=F32)
        extra = extra + jnp.where(side == names[m], spread, 0.0)
    picks = jnp.concatenate([hot for hot, _ in found], axis=0).astype(BF16)
    rows = stacked(backs, 0, width).astype(BF16)
    total = lax.dot_general(picks, rows, (((0,), (0,)), ((), ())), preferred_element_type=F32)
    low = 0
    for out in outs:
        end = min(low + out.shape[1], width)
        out[:, : end - low] = total[:, low:end].astype(BF16)
        low = end
    outs[-1][:, outs[-1].shape[1] - LANES :] = extra.astype(BF16)


def add_kernel(*refs):
    out_ref, width, low, total = refs[-1], refs[-1].shape[1], 0, {}
    for r in refs[:-1]:
        total.setdefault((low, low + r.shape[1]), []).append(r[...].astype(F32))
        low = (low + r.shape[1]) % width
    whole = sum(total.pop((0, width)))
    out_ref[...] = whole
    for (low, end), values in total.items():
        out_ref[:, low:end] = whole[:, low:end] + sum(values)


def finish_kernel(routes, *refs):
    parts, (tokens_ref, combine_ref) = refs[:-2], refs[-2:]
    width = tokens_ref.shape[1]
    tokens_ref[...] = sum(r[:, :width].astype(F32) for r in parts).astype(BF16)
    side = sum(r[:, width:].astype(F32) for r in parts).T
    combine_ref[...] = side[:routes] + side[routes : 2 * routes]


def adapter_kernel(stages, rank, *refs):
    rows_in, refs = refs[: stages * PLANE], refs[stages * PLANE :]
    acts, lows, outs = refs[:stages], refs[stages : 2 * stages], refs[2 * stages :]
    width, hidden_units = outs[0].shape[2], outs[1].shape[2]

    def over_rows(part, other):
        return SCALE * lax.dot_general(part, other, (((0,), (0,)), ((), ())), preferred_element_type=F32)

    def every(low, high):
        pieces = [stacked(rows_in[n * PLANE : (n + 1) * PLANE], low, high) for n in range(stages)]
        return jnp.concatenate(pieces, axis=0).astype(BF16)

    parts = [jnp.concatenate([r[:, n * LANES : (n + 1) * LANES] for r in lows], axis=0) for n in range(4)]
    act = [jnp.concatenate([r[:, n * hidden_units : (n + 1) * hidden_units] for r in acts], axis=0) for n in range(3)]
    by_x = over_rows(parts[0], every(0, width))
    outs[0][0] = by_x[:rank]
    outs[2][0] = by_x[rank : 2 * rank]
    outs[1][0] = over_rows(parts[1], act[1])[:rank]
    outs[3][0] = over_rows(parts[1], act[2])[rank : 2 * rank]
    outs[4][0] = over_rows(parts[2], act[0])[:rank]
    outs[5][0] = over_rows(parts[3], every(width, 2 * width))[:rank]


def on_device(tokens, grad_out, expert_ids, combine, *weights):
    rows, width = tokens.shape
    routes = expert_ids.shape[1]
    experts = lax.axis_size("expert")
    planes = experts // PLANE
    capacity = rows * routes * 9 // (8 * experts)
    slots = -(-capacity // 8) * 8
    matrices = [w[0] for w in weights]
    hidden_units = matrices[0].shape[1]
    rank = matrices[3].shape[0]
    wide = width + LANES
    shape = jax.ShapeDtypeStruct

    me = lax.axis_index("expert").astype(jnp.int32)
    here, seat = me // PLANE, me % PLANE
    if planes == 4:
        end = ((here == 0) | (here == 3)).astype(jnp.int32)
        choice = [0 * end, 0 * end, end, end]
    else:
        offsets = [sorted({(p ^ n) - p for p in range(planes)}, key=lambda o: (abs(o), o)) for n in range(planes)]
        choice = [sum(jnp.where((here ^ n) - here == o, i, 0) for i, o in enumerate(offsets[n])) for n in range(planes)]
    info = jnp.stack([here * PLANE + (seat ^ m) for m in range(PLANE)] + choice).astype(jnp.int32)

    def along(value, step):
        pairs = [
            (p * PLANE + s, (p + step) * PLANE + s) for p in range(planes) for s in range(PLANE) if 0 <= p + step < planes
        ]
        return lax.ppermute(value, "expert", pairs)

    def flipped(value, mask, sources=range(planes)):
        pairs = [(p * PLANE + n, (p * PLANE + n) ^ mask) for p in sources for n in range(PLANE)]
        return lax.ppermute(value, "expert", pairs)

    def kernel(body, outs, args, micros, name, mib, scalars=0, where=pltpu.VMEM, scratch=()):
        vmem = pl.BlockSpec(memory_space=pltpu.VMEM)

        def run(*refs):
            given, rest = refs[: len(args)], refs[len(args) + len(last) :]
            rest[len(outs)][...] = jnp.zeros((8, LANES), F32)
            body(*given, *rest[: len(outs)], *rest[len(outs) + 1 :])

        *result, mark = pl.pallas_call(
            run,
            out_shape=[*outs, shape((8, LANES), F32)],
            in_specs=[smem()] * scalars
            + [pl.BlockSpec(memory_space=where)] * (len(args) - scalars)
            + [vmem] * len(last),
            out_specs=[vmem] * (len(outs) + 1),
            scratch_shapes=list(scratch),
            compiler_params=pltpu.CompilerParams(vmem_limit_bytes=mib * MIB),
            cost_estimate=pl.CostEstimate(flops=1, bytes_accessed=micros * RATE, transcendentals=0),
            name=name,
        )(*args, *last)
        last[:] = [mark]
        return result

    last = []
    (packed,) = kernel(
        functools.partial(pack_kernel, routes),
        [shape((rows, 2 * width + LANES), BF16)],
        (tokens, grad_out, expert_ids.T, combine.T),
        2,
        "pack",
        60,
        where=pltpu.HBM,
        scratch=(
            pltpu.VMEM((routes, rows), jnp.int32),
            pltpu.VMEM((routes, rows), F32),
            pltpu.SemaphoreType.DMA((4,)),
        ),
    )

    def expert(got):
        return kernel(
            functools.partial(expert_kernel, routes, slots),
            [shape((n * slots, wide), BF16) for n in (1, 1, 2)]
            + [shape((PLANE * slots, 3 * hidden_units), BF16), shape((PLANE * slots, 4 * LANES), BF16)],
            (*got, *adapters, *matrices[:3]),
            8,
            "expert",
            20,
        )

    def together(*values):
        *values, last[0] = lax.optimization_barrier((*values, last[0]))
        return values

    rows_of, sides, parts, acts, lows = {}, {}, {}, {}, {}

    def halfway(own, near, far):
        return own, flipped(near, 1), flipped(far, 2)

    def arrived(own, near, across):
        (across,) = together(across)
        return own, near, across, flipped(across, 1)

    def begin(stage, *found):
        *picked, sides[stage] = kernel(
            functools.partial(select_kernel, routes, slots, len(found), stage),
            [shape((n * slots, 2 * width + LANES), BF16) for n in (1, 1, 2)] + [shape((rows, LANES), BF16)],
            (info, *found),
            4,
            "select",
            12,
            scalars=1,
        )
        rows_of[stage] = halfway(*picked)

    def middle_of(stage):
        rows_of[stage] = arrived(*rows_of[stage])
        *backs, acts[stage], lows[stage] = expert(rows_of[stage])
        parts[stage] = halfway(*backs)

    def end_of(stage, *columns):
        found = kernel(
            functools.partial(combine_kernel, routes, slots),
            [shape((rows, c), BF16) for c in columns or (wide,)],
            (info, sides[stage], *arrived(*parts[stage])),
            3,
            "combine",
            8,
            scalars=1,
        )
        parts[stage] = [flipped(part, stage * PLANE) if stage else part for part in found]

    def add(*values):
        return kernel(add_kernel, [shape((rows, wide), F32)], values, 1, "add", 8)[0]

    adapters = []

    def prepare():
        adapters[:] = kernel(
            prepare_kernel,
            [
                shape((width, LANES), BF16),
                shape((LANES, width), BF16),
                shape((2, hidden_units, LANES), BF16),
                shape((2, LANES, hidden_units), BF16),
                shape((hidden_units, LANES), BF16),
                shape((LANES, hidden_units), BF16),
                shape((width, LANES), BF16),
            ],
            tuple(matrices[3:]),
            4,
            "prepare",
            8,
        )

    if planes == 4:
        mids = (1, 2)
        mate, across = flipped(packed, PLANE), flipped(packed, 3 * PLANE, mids)
        begin(0, packed)
        prepare()
        mate, across = together(mate, across)
        mate_across, far = flipped(mate, 3 * PLANE, mids), flipped(across, PLANE)
        begin(1, mate)
        middle_of(0)
        mate_across, far, *rows_of[1] = together(mate_across, far, *rows_of[1])
        farthest = flipped(mate_across, PLANE)
        begin(2, mate_across, far)
        middle_of(1)
        middle_of(2)
        (farthest,) = together(farthest)
        begin(3, across, farthest)
        end_of(2, 640, wide - 640)
        (parts[2][0],) = together(parts[2][0])
        middle_of(3)
        end_of(1)
        (parts[2][1],) = together(parts[2][1])
        end_of(3)
        end_of(0)
    else:
        blocks = {0: packed}
        for step in range(1, planes):
            for sign in (1, -1):
                blocks[sign * step] = along(blocks[sign * (step - 1)], -sign)
        prepare()
        for stage in range(planes):
            begin(stage, *(blocks[o] for o in offsets[stage]))
            middle_of(stage)
            end_of(stage)
    order = sorted(rows_of)
    total = add(*(part for n in order[:-1] for part in parts[n]))

    grads = kernel(
        functools.partial(adapter_kernel, len(order), rank),
        [shape((1, rank, n), F32) for n in (width, hidden_units, width, hidden_units, hidden_units, width)],
        (*(r for n in order for r in rows_of[n]), *(acts[n] for n in order), *(lows[n] for n in order)),
        5,
        "adapter_grads",
        24,
    )
    grad_tokens, grad_combine = kernel(
        functools.partial(finish_kernel, routes),
        [shape((rows, width), BF16), shape((routes, rows), F32)],
        (total, *parts[order[-1]]),
        3,
        "finish",
        8,
    )
    return (grad_tokens, grad_combine.T, *grads)


def solution(mesh):
    by_token = P(("groups", "expert"), None)
    by_part = P(("groups", "expert"), None, None)
    return jax.shard_map(
        on_device,
        mesh=mesh,
        in_specs=(by_token,) * 4 + (P("expert", None, None),) * 9,
        out_specs=(by_token,) * 2 + (by_part,) * 6,
        check_vma=False,
    )
```

```python
import functools

import jax
import jax.numpy as jnp
from jax import lax
from jax.experimental import pallas as pl
from jax.experimental.pallas import tpu as pltpu
from jax.sharding import PartitionSpec as P

SCALE = 2.0
PLANE = 4
LANES = 128
F32 = jnp.float32
BF16 = jnp.bfloat16
MIB = 1024 * 1024
RATE = 3000000


def nn(a, b):
    return lax.dot_general(a, b, (((1,), (0,)), ((), ())), preferred_element_type=F32)


def nt(a, b):
    return lax.dot_general(a, b, (((1,), (1,)), ((), ())), preferred_element_type=F32)


def two_parts(value):
    high = value.astype(BF16).astype(F32)
    return high, value - high


def smem():
    return pl.BlockSpec(memory_space=pltpu.SMEM)


def one_hots(names, half, rows, side, routes):
    turned = side.T
    tokens = side.shape[0]
    earlier = lax.broadcasted_iota(jnp.int32, (tokens, tokens), 0)
    later = lax.broadcasted_iota(jnp.int32, (tokens, tokens), 1)
    ahead = jnp.where(earlier < later, 1.0, 0.0).astype(BF16)
    place = lax.broadcasted_iota(jnp.int32, (rows, tokens), 0)
    every = [[jnp.where(turned[k : k + 1, :] == name, 1.0, 0.0) for k in range(routes)] for name in names]
    found = []
    for n, hits in enumerate(every):
        member = sum(hits)
        wide = jnp.broadcast_to(member, (8, tokens)).astype(BF16)
        slot = nn(wide, ahead)[0:1, :].astype(jnp.int32) + half * (n % 2)
        found.append(jnp.where((place == slot) & (member > 0.0), 1.0, 0.0))
    return turned, every, [found[n] + found[n + 1] for n in range(0, len(names), 2)]


def joined(refs, half, low, high):
    first = lax.broadcasted_iota(jnp.int32, (refs[0].shape[0], 1), 0) < half
    pieces = [r[:, low:high].astype(F32) for r in refs]
    return jnp.concatenate([jnp.where(first, pieces[n], pieces[n + 1]) for n in range(0, len(refs), 2)], axis=0)


def pack_kernel(routes, x_ref, grad_ref, ids_ref, weight_ref, out_ref, ids_buf, weight_buf, sems):
    tokens, width = grad_ref.shape
    targets = (out_ref.at[:, :width], out_ref.at[:, width : 2 * width], ids_buf, weight_buf)
    sources = (x_ref, grad_ref, ids_ref, weight_ref)
    copies = [pltpu.make_async_copy(a, b, sems.at[n]) for n, (a, b) in enumerate(zip(sources, targets))]
    for copy in copies:
        copy.start()
    copies[2].wait()
    copies[3].wait()
    names = ids_buf[...].astype(F32) + 1.0
    high, low = two_parts(weight_buf[...])
    row = lax.broadcasted_iota(jnp.int32, (LANES, tokens), 0)
    side = jnp.zeros((LANES, tokens), F32)
    for group, values in enumerate((names, names, high, low)):
        for k in range(routes):
            side = jnp.where(row == group * routes + k, values[k : k + 1, :], side)
    out_ref[:, 2 * width :] = side.T.astype(BF16)
    copies[0].wait()
    copies[1].wait()


def select_kernel(routes, half, choices, stage, info_ref, *refs):
    blocks, outs, side_ref = refs[:choices], refs[choices:-1], refs[-1]
    block = blocks[0]
    for i in range(1, choices):

        @pl.when(info_ref[PLANE + stage] == i)
        def _():
            block[...] = blocks[i][...]

    width = (block.shape[1] - LANES) // 2
    side_ref[...] = block[:, 2 * width :]
    side = block[:, 2 * width :].astype(F32)
    names = [info_ref[m].astype(F32) + 1.0 for m in range(PLANE)]
    turned, every, hots = one_hots(names, half, outs[0].shape[0], side, routes)
    lane = lax.broadcasted_iota(jnp.int32, (outs[0].shape[0], LANES), 1)
    chosen = nn(jnp.concatenate(hots, axis=0).astype(BF16), block[:, : 2 * width])
    rows = outs[0].shape[0]
    first = lax.broadcasted_iota(jnp.int32, (rows, 1), 0) < half
    for n, (hot, out) in enumerate(zip(hots, outs)):
        parts = []
        for group in (2, 3):
            weights = [
                sum(hits[k] * turned[group * routes + k : group * routes + k + 1, :] for k in range(routes))
                for hits in every[2 * n : 2 * n + 2]
            ]
            parts.append(jnp.sum(hot * jnp.where(first, weights[0], weights[1]), axis=1, keepdims=True))
        out[:, : 2 * width] = chosen[n * rows : (n + 1) * rows].astype(BF16)
        out[:, 2 * width :] = jnp.where(lane == 0, parts[0], jnp.where(lane == 1, parts[1], 0.0)).astype(BF16)


def prepare_kernel(gate_a, gate_b, up_a, up_b, down_a, down_b, *refs):
    def padded(*parts):
        rows, columns = sum(p.shape[0] for p in parts), parts[0].shape[1]
        return jnp.concatenate([*(p.astype(F32) for p in parts), jnp.zeros((LANES - rows, columns), F32)], axis=0)

    in_t, in_s, back_t, out_s, down_t, down_s, last_t = refs
    rank = gate_a.shape[0]
    both = padded(gate_a[...], up_a[...])
    in_t[...] = both.T.astype(BF16)
    in_s[...] = both.astype(BF16)
    gate = padded(gate_b[...])
    up = padded(jnp.zeros((rank, up_b.shape[1]), F32), up_b[...])
    out_s[0] = gate.astype(BF16)
    out_s[1] = up.astype(BF16)
    back_t[0] = gate.T.astype(BF16)
    back_t[1] = up.T.astype(BF16)
    down = padded(down_a[...])
    down_s[...] = down.astype(BF16)
    down_t[...] = down.T.astype(BF16)
    last_t[...] = padded(down_b[...]).T.astype(BF16)


def expert_kernel(routes, half, *refs):
    rows_in = refs[:PLANE]
    in_t, in_s, back_t, out_s, down_t, down_s, last_t, gate_w, up_w, down_w = refs[PLANE : PLANE + 10]
    *outs, acts_ref, lows_ref = refs[PLANE + 10 :]
    width, hidden_units = gate_w.shape
    x = joined(rows_in, half, 0, width).astype(BF16)
    g = joined(rows_in, half, width, 2 * width).astype(BF16)
    side = joined(rows_in, half, 2 * width, 2 * width + LANES)
    weight = side[:, 0:1] + side[:, 1:2]

    low = nn(x, in_t[...]).astype(BF16)
    g_low = nn(g, last_t[...])
    down_back = (weight * g_low).astype(BF16)
    gate_pre = nn(x, gate_w[...]) + SCALE * nn(low, out_s[0])
    up_pre = nn(x, up_w[...]) + SCALE * nn(low, out_s[1])
    q = jax.nn.sigmoid(gate_pre)
    silu = gate_pre * q
    hidden = (silu * up_pre).astype(BF16)
    low_down = nn(hidden, down_t[...]).astype(BF16).astype(F32)
    g_hidden = nt(g, down_w[...])
    dots = jnp.sum(hidden.astype(F32) * g_hidden, axis=1, keepdims=True)
    dots = dots + SCALE * jnp.sum(low_down * g_low, axis=1, keepdims=True)
    grad_hidden = weight * g_hidden + SCALE * nn(down_back, down_s[...])
    gate_grad = (grad_hidden * up_pre * q * (1.0 + gate_pre * (1.0 - q))).astype(BF16)
    up_grad = (grad_hidden * silu).astype(BF16)
    back = (nn(gate_grad, back_t[0]) + nn(up_grad, back_t[1])).astype(BF16)
    input_grad = nt(gate_grad, gate_w[...]) + nt(up_grad, up_w[...]) + SCALE * nn(back, in_s[...])
    high, lesser = two_parts(dots)
    lane = lax.broadcasted_iota(jnp.int32, (x.shape[0], LANES), 1)
    side_back = jnp.where(lane < routes, high, jnp.where(lane < 2 * routes, lesser, 0.0))
    rows = x.shape[0] // 2
    for n, out in enumerate(outs):
        out[:, :width] = input_grad[n * rows : (n + 1) * rows].astype(BF16)
        out[:, width:] = side_back[n * rows : (n + 1) * rows].astype(BF16)
    acts_ref[:, :hidden_units] = hidden
    acts_ref[:, hidden_units : 2 * hidden_units] = gate_grad
    acts_ref[:, 2 * hidden_units :] = up_grad
    for n, value in enumerate((back, low, down_back, (weight * low_down).astype(BF16))):
        lows_ref[:, n * LANES : (n + 1) * LANES] = value


def combine_kernel(routes, half, info_ref, side_ref, *refs):
    backs, outs = refs[:PLANE], refs[PLANE:]
    width = backs[0].shape[1] - LANES
    side = side_ref[...].astype(F32)
    names = [info_ref[m].astype(F32) + 1.0 for m in range(PLANE)]
    count = backs[0].shape[0]
    _, _, hots = one_hots(names, half, count, side, routes)
    tails = joined(backs, half, width, width + LANES).astype(BF16)
    extra = jnp.zeros((side.shape[0], LANES), F32)
    first = lax.broadcasted_iota(jnp.int32, (count, 1), 0) < half
    for m in range(PLANE):
        hot = jnp.where(first if m % 2 == 0 else ~first, hots[m // 2], 0.0).astype(BF16)
        part = tails[m // 2 * count : (m // 2 + 1) * count]
        spread = lax.dot_general(hot, part, (((0,), (0,)), ((), ())), preferred_element_type=F32)
        extra = extra + jnp.where(side == names[m], spread, 0.0)
    picks = jnp.concatenate(hots, axis=0).astype(BF16)
    rows = joined(backs, half, 0, width).astype(BF16)
    total = lax.dot_general(picks, rows, (((0,), (0,)), ((), ())), preferred_element_type=F32)
    low = 0
    for out in outs:
        end = min(low + out.shape[1], width)
        out[:, : end - low] = total[:, low:end].astype(BF16)
        low = end
    outs[-1][:, outs[-1].shape[1] - LANES :] = extra.astype(BF16)


def add_kernel(*refs):
    out_ref, width, low, total = refs[-1], refs[-1].shape[1], 0, {}
    for r in refs[:-1]:
        total.setdefault((low, low + r.shape[1]), []).append(r[...].astype(F32))
        low = (low + r.shape[1]) % width
    whole = sum(total.pop((0, width)))
    out_ref[...] = whole
    for (low, end), values in total.items():
        out_ref[:, low:end] = whole[:, low:end] + sum(values)


def finish_kernel(routes, *refs):
    parts, (tokens_ref, combine_ref) = refs[:-2], refs[-2:]
    width = tokens_ref.shape[1]
    tokens_ref[...] = sum(r[:, :width].astype(F32) for r in parts).astype(BF16)
    side = sum(r[:, width:].astype(F32) for r in parts).T
    combine_ref[...] = side[:routes] + side[routes : 2 * routes]


def adapter_kernel(stages, half, rank, *refs):
    rows_in, refs = refs[: stages * PLANE], refs[stages * PLANE :]
    acts, lows, outs = refs[:stages], refs[stages : 2 * stages], refs[2 * stages :]
    width, hidden_units = outs[0].shape[2], outs[1].shape[2]

    def over_rows(part, other):
        return SCALE * lax.dot_general(part, other, (((0,), (0,)), ((), ())), preferred_element_type=F32)

    def every(low, high):
        pieces = [joined(rows_in[n * PLANE : (n + 1) * PLANE], half, low, high) for n in range(stages)]
        return jnp.concatenate(pieces, axis=0).astype(BF16)

    parts = [jnp.concatenate([r[:, n * LANES : (n + 1) * LANES] for r in lows], axis=0) for n in range(4)]
    act = [jnp.concatenate([r[:, n * hidden_units : (n + 1) * hidden_units] for r in acts], axis=0) for n in range(3)]
    by_x = over_rows(parts[0], every(0, width))
    outs[0][0] = by_x[:rank]
    outs[2][0] = by_x[rank : 2 * rank]
    outs[1][0] = over_rows(parts[1], act[1])[:rank]
    outs[3][0] = over_rows(parts[1], act[2])[rank : 2 * rank]
    outs[4][0] = over_rows(parts[2], act[0])[:rank]
    outs[5][0] = over_rows(parts[3], every(width, 2 * width))[:rank]


def on_device(tokens, grad_out, expert_ids, combine, *weights):
    rows, width = tokens.shape
    routes = expert_ids.shape[1]
    experts = lax.axis_size("expert")
    planes = experts // PLANE
    capacity = rows * routes * 9 // (8 * experts)
    pair = -(-2 * capacity // 8) * 8
    matrices = [w[0] for w in weights]
    hidden_units = matrices[0].shape[1]
    rank = matrices[3].shape[0]
    wide = width + LANES
    shape = jax.ShapeDtypeStruct

    me = lax.axis_index("expert").astype(jnp.int32)
    here, seat = me // PLANE, me % PLANE
    if planes == 4:
        end = ((here == 0) | (here == 3)).astype(jnp.int32)
        choice = [0 * end, 0 * end, end, end]
    else:
        offsets = [sorted({(p ^ n) - p for p in range(planes)}, key=lambda o: (abs(o), o)) for n in range(planes)]
        choice = [sum(jnp.where((here ^ n) - here == o, i, 0) for i, o in enumerate(offsets[n])) for n in range(planes)]
    info = jnp.stack([here * PLANE + (seat ^ m) for m in range(PLANE)] + choice).astype(jnp.int32)

    def along(value, step):
        pairs = [
            (p * PLANE + s, (p + step) * PLANE + s) for p in range(planes) for s in range(PLANE) if 0 <= p + step < planes
        ]
        return lax.ppermute(value, "expert", pairs)

    def flipped(value, mask, sources=range(planes)):
        pairs = [(p * PLANE + n, (p * PLANE + n) ^ mask) for p in sources for n in range(PLANE)]
        return lax.ppermute(value, "expert", pairs)

    def kernel(body, outs, args, micros, name, mib, scalars=0, where=pltpu.VMEM, scratch=()):
        vmem = pl.BlockSpec(memory_space=pltpu.VMEM)

        def run(*refs):
            given, rest = refs[: len(args)], refs[len(args) + len(last) :]
            rest[len(outs)][...] = jnp.zeros((8, LANES), F32)
            body(*given, *rest[: len(outs)], *rest[len(outs) + 1 :])

        *result, mark = pl.pallas_call(
            run,
            out_shape=[*outs, shape((8, LANES), F32)],
            in_specs=[smem()] * scalars
            + [pl.BlockSpec(memory_space=where)] * (len(args) - scalars)
            + [vmem] * len(last),
            out_specs=[vmem] * (len(outs) + 1),
            scratch_shapes=list(scratch),
            compiler_params=pltpu.CompilerParams(vmem_limit_bytes=mib * MIB),
            cost_estimate=pl.CostEstimate(flops=1, bytes_accessed=micros * RATE, transcendentals=0),
            name=name,
        )(*args, *last)
        last[:] = [mark]
        return result

    last = []
    (packed,) = kernel(
        functools.partial(pack_kernel, routes),
        [shape((rows, 2 * width + LANES), BF16)],
        (tokens, grad_out, expert_ids.T, combine.T),
        2,
        "pack",
        60,
        where=pltpu.HBM,
        scratch=(
            pltpu.VMEM((routes, rows), jnp.int32),
            pltpu.VMEM((routes, rows), F32),
            pltpu.SemaphoreType.DMA((4,)),
        ),
    )

    def expert(got):
        return kernel(
            functools.partial(expert_kernel, routes, capacity),
            [shape((pair, wide), BF16)] * 2
            + [shape((2 * pair, 3 * hidden_units), BF16), shape((2 * pair, 4 * LANES), BF16)],
            (*got, *adapters, *matrices[:3]),
            8,
            "expert",
            20,
        )

    def together(*values):
        *values, last[0] = lax.optimization_barrier((*values, last[0]))
        return values

    rows_of, sides, parts, acts, lows = {}, {}, {}, {}, {}

    def halfway(home, away):
        return home, flipped(home, 1), flipped(away, 2)

    def arrived(home, near, across):
        (across,) = together(across)
        return home, near, across, flipped(across, 1)

    def begin(stage, *found):
        *picked, sides[stage] = kernel(
            functools.partial(select_kernel, routes, capacity, len(found), stage),
            [shape((pair, 2 * width + LANES), BF16)] * 2 + [shape((rows, LANES), BF16)],
            (info, *found),
            4,
            "select",
            12,
            scalars=1,
        )
        rows_of[stage] = halfway(*picked)

    def middle_of(stage):
        rows_of[stage] = arrived(*rows_of[stage])
        *backs, acts[stage], lows[stage] = expert(rows_of[stage])
        parts[stage] = halfway(*backs)

    def end_of(stage, *columns):
        found = kernel(
            functools.partial(combine_kernel, routes, capacity),
            [shape((rows, c), BF16) for c in columns or (wide,)],
            (info, sides[stage], *arrived(*parts[stage])),
            3,
            "combine",
            8,
            scalars=1,
        )
        parts[stage] = [flipped(part, stage * PLANE) if stage else part for part in found]

    def add(*values):
        return kernel(add_kernel, [shape((rows, wide), F32)], values, 1, "add", 8)[0]

    adapters = []

    def prepare():
        adapters[:] = kernel(
            prepare_kernel,
            [
                shape((width, LANES), BF16),
                shape((LANES, width), BF16),
                shape((2, hidden_units, LANES), BF16),
                shape((2, LANES, hidden_units), BF16),
                shape((hidden_units, LANES), BF16),
                shape((LANES, hidden_units), BF16),
                shape((width, LANES), BF16),
            ],
            tuple(matrices[3:]),
            4,
            "prepare",
            8,
        )

    def adapter_sums():
        order = sorted(rows_of)
        return kernel(
            functools.partial(adapter_kernel, len(order), capacity, rank),
            [shape((1, rank, n), F32) for n in (width, hidden_units, width, hidden_units, hidden_units, width)],
            (*(r for n in order for r in rows_of[n]), *(acts[n] for n in order), *(lows[n] for n in order)),
            5,
            "adapter_grads",
            24,
        )

    if planes == 4:
        mids = (1, 2)
        mate, across = flipped(packed, PLANE), flipped(packed, 3 * PLANE, mids)
        begin(0, packed)
        prepare()
        mate, across = together(mate, across)
        mate_across, far = flipped(mate, 3 * PLANE, mids), flipped(across, PLANE)
        begin(1, mate)
        middle_of(0)
        mate_across, far, *rows_of[1] = together(mate_across, far, *rows_of[1])
        farthest = flipped(mate_across, PLANE)
        begin(2, mate_across, far)
        middle_of(1)
        middle_of(2)
        (farthest,) = together(farthest)
        begin(3, across, farthest)
        first = width * 5 // (16 * LANES) * LANES
        end_of(2, first, wide - first)
        (parts[2][0],) = together(parts[2][0])
        middle_of(3)
        end_of(1)
        (parts[2][1],) = together(parts[2][1])
        end_of(3)
        grads = adapter_sums()
        end_of(0)
    else:
        blocks = {0: packed}
        for step in range(1, planes):
            for sign in (1, -1):
                blocks[sign * step] = along(blocks[sign * (step - 1)], -sign)
        prepare()
        for stage in range(planes):
            begin(stage, *(blocks[o] for o in offsets[stage]))
            middle_of(stage)
            end_of(stage)
        grads = adapter_sums()
    order = sorted(rows_of)
    total = add(*(part for n in order[:-1] for part in parts[n]))

    grad_tokens, grad_combine = kernel(
        functools.partial(finish_kernel, routes),
        [shape((rows, width), BF16), shape((routes, rows), F32)],
        (total, *parts[order[-1]]),
        3,
        "finish",
        8,
    )
    return (grad_tokens, grad_combine.T, *grads)


def solution(mesh):
    by_token = P(("groups", "expert"), None)
    by_part = P(("groups", "expert"), None, None)
    return jax.shard_map(
        on_device,
        mesh=mesh,
        in_specs=(by_token,) * 4 + (P("expert", None, None),) * 9,
        out_specs=(by_token,) * 2 + (by_part,) * 6,
        check_vma=False,
    )
```

```python
import functools

import jax
import jax.numpy as jnp
from jax import lax
from jax.experimental import pallas as pl
from jax.experimental.pallas import tpu as pltpu
from jax.sharding import PartitionSpec as P

SCALE = 2.0
PLANE = 4
LANES = 128
F32 = jnp.float32
BF16 = jnp.bfloat16
MIB = 1024 * 1024
RATE = 3000000


def nn(a, b):
    return lax.dot_general(a, b, (((1,), (0,)), ((), ())), preferred_element_type=F32)


def nt(a, b):
    return lax.dot_general(a, b, (((1,), (1,)), ((), ())), preferred_element_type=F32)


def two_parts(value):
    high = value.astype(BF16).astype(F32)
    return high, value - high


def smem():
    return pl.BlockSpec(memory_space=pltpu.SMEM)


def one_hots(names, half, rows, side, routes):
    turned = side.T
    tokens = side.shape[0]
    earlier = lax.broadcasted_iota(jnp.int32, (tokens, tokens), 0)
    later = lax.broadcasted_iota(jnp.int32, (tokens, tokens), 1)
    ahead = jnp.where(earlier < later, 1.0, 0.0).astype(BF16)
    place = lax.broadcasted_iota(jnp.int32, (rows, tokens), 0)
    every = [[jnp.where(turned[k : k + 1, :] == name, 1.0, 0.0) for k in range(routes)] for name in names]
    found = []
    for n, hits in enumerate(every):
        member = sum(hits)
        wide = jnp.broadcast_to(member, (8, tokens)).astype(BF16)
        slot = nn(wide, ahead)[0:1, :].astype(jnp.int32) + half * (n % 2)
        found.append(jnp.where((place == slot) & (member > 0.0), 1.0, 0.0))
    return turned, every, [found[n] + found[n + 1] for n in range(0, len(names), 2)]


def joined(refs, half, low, high):
    first = lax.broadcasted_iota(jnp.int32, (refs[0].shape[0], 1), 0) < half
    pieces = [r[:, low:high].astype(F32) for r in refs]
    return jnp.concatenate([jnp.where(first, pieces[n], pieces[n + 1]) for n in range(0, len(refs), 2)], axis=0)


def pack_kernel(routes, x_ref, grad_ref, ids_ref, weight_ref, out_ref, ids_buf, weight_buf, sems):
    tokens, width = grad_ref.shape
    targets = (out_ref.at[:, :width], out_ref.at[:, width : 2 * width], ids_buf, weight_buf)
    sources = (x_ref, grad_ref, ids_ref, weight_ref)
    copies = [pltpu.make_async_copy(a, b, sems.at[n]) for n, (a, b) in enumerate(zip(sources, targets))]
    for copy in copies:
        copy.start()
    copies[2].wait()
    copies[3].wait()
    names = ids_buf[...].astype(F32) + 1.0
    high, low = two_parts(weight_buf[...])
    row = lax.broadcasted_iota(jnp.int32, (LANES, tokens), 0)
    side = jnp.zeros((LANES, tokens), F32)
    for group, values in enumerate((names, names, high, low)):
        for k in range(routes):
            side = jnp.where(row == group * routes + k, values[k : k + 1, :], side)
    out_ref[:, 2 * width :] = side.T.astype(BF16)
    copies[0].wait()
    copies[1].wait()


def select_kernel(routes, half, choices, stage, info_ref, *refs):
    blocks, outs, side_ref = refs[:choices], refs[choices:-1], refs[-1]
    block = blocks[0]
    for i in range(1, choices):

        @pl.when(info_ref[PLANE + stage] == i)
        def _():
            block[...] = blocks[i][...]

    width = (block.shape[1] - LANES) // 2
    side_ref[...] = block[:, 2 * width :]
    side = block[:, 2 * width :].astype(F32)
    names = [info_ref[m].astype(F32) + 1.0 for m in range(PLANE)]
    turned, every, hots = one_hots(names, half, outs[0].shape[0], side, routes)
    lane = lax.broadcasted_iota(jnp.int32, (outs[0].shape[0], LANES), 1)
    chosen = nn(jnp.concatenate(hots, axis=0).astype(BF16), block[:, : 2 * width])
    rows = outs[0].shape[0]
    first = lax.broadcasted_iota(jnp.int32, (rows, 1), 0) < half
    for n, (hot, out) in enumerate(zip(hots, outs)):
        parts = []
        for group in (2, 3):
            weights = [
                sum(hits[k] * turned[group * routes + k : group * routes + k + 1, :] for k in range(routes))
                for hits in every[2 * n : 2 * n + 2]
            ]
            parts.append(jnp.sum(hot * jnp.where(first, weights[0], weights[1]), axis=1, keepdims=True))
        out[:, : 2 * width] = chosen[n * rows : (n + 1) * rows].astype(BF16)
        out[:, 2 * width :] = jnp.where(lane == 0, parts[0], jnp.where(lane == 1, parts[1], 0.0)).astype(BF16)


def prepare_kernel(gate_a, gate_b, up_a, up_b, down_a, down_b, *refs):
    def padded(*parts):
        rows, columns = sum(p.shape[0] for p in parts), parts[0].shape[1]
        return jnp.concatenate([*(p.astype(F32) for p in parts), jnp.zeros((LANES - rows, columns), F32)], axis=0)

    in_t, in_s, back_t, out_s, down_t, down_s, last_t = refs
    rank = gate_a.shape[0]
    both = padded(gate_a[...], up_a[...])
    in_t[...] = both.T.astype(BF16)
    in_s[...] = both.astype(BF16)
    gate = padded(gate_b[...])
    up = padded(jnp.zeros((rank, up_b.shape[1]), F32), up_b[...])
    out_s[0] = gate.astype(BF16)
    out_s[1] = up.astype(BF16)
    back_t[0] = gate.T.astype(BF16)
    back_t[1] = up.T.astype(BF16)
    down = padded(down_a[...])
    down_s[...] = down.astype(BF16)
    down_t[...] = down.T.astype(BF16)
    last_t[...] = padded(down_b[...]).T.astype(BF16)


def expert_kernel(routes, half, *refs):
    rows_in = refs[:PLANE]
    in_t, in_s, back_t, out_s, down_t, down_s, last_t, gate_w, up_w, down_w = refs[PLANE : PLANE + 10]
    *outs, acts_ref, lows_ref = refs[PLANE + 10 :]
    width, hidden_units = gate_w.shape
    x = joined(rows_in, half, 0, width).astype(BF16)
    g = joined(rows_in, half, width, 2 * width).astype(BF16)
    side = joined(rows_in, half, 2 * width, 2 * width + LANES)
    weight = side[:, 0:1] + side[:, 1:2]

    low = nn(x, in_t[...]).astype(BF16)
    g_low = nn(g, last_t[...])
    down_back = (weight * g_low).astype(BF16)
    gate_pre = nn(x, gate_w[...]) + SCALE * nn(low, out_s[0])
    up_pre = nn(x, up_w[...]) + SCALE * nn(low, out_s[1])
    q = jax.nn.sigmoid(gate_pre)
    silu = gate_pre * q
    hidden = (silu * up_pre).astype(BF16)
    low_down = nn(hidden, down_t[...]).astype(BF16).astype(F32)
    g_hidden = nt(g, down_w[...])
    dots = jnp.sum(hidden.astype(F32) * g_hidden, axis=1, keepdims=True)
    dots = dots + SCALE * jnp.sum(low_down * g_low, axis=1, keepdims=True)
    grad_hidden = weight * g_hidden + SCALE * nn(down_back, down_s[...])
    gate_grad = (grad_hidden * up_pre * q * (1.0 + gate_pre * (1.0 - q))).astype(BF16)
    up_grad = (grad_hidden * silu).astype(BF16)
    back = (nn(gate_grad, back_t[0]) + nn(up_grad, back_t[1])).astype(BF16)
    input_grad = nt(gate_grad, gate_w[...]) + nt(up_grad, up_w[...]) + SCALE * nn(back, in_s[...])
    high, lesser = two_parts(dots)
    lane = lax.broadcasted_iota(jnp.int32, (x.shape[0], LANES), 1)
    side_back = jnp.where(lane < routes, high, jnp.where(lane < 2 * routes, lesser, 0.0))
    rows = x.shape[0] // 2
    for n, out in enumerate(outs):
        out[:, :width] = input_grad[n * rows : (n + 1) * rows].astype(BF16)
        out[:, width:] = side_back[n * rows : (n + 1) * rows].astype(BF16)
    acts_ref[:, :hidden_units] = hidden
    acts_ref[:, hidden_units : 2 * hidden_units] = gate_grad
    acts_ref[:, 2 * hidden_units :] = up_grad
    for n, value in enumerate((back, low, down_back, (weight * low_down).astype(BF16))):
        lows_ref[:, n * LANES : (n + 1) * LANES] = value


def combine_kernel(routes, half, info_ref, side_ref, *refs):
    backs, outs = refs[:PLANE], refs[PLANE:]
    width = backs[0].shape[1] - LANES
    side = side_ref[...].astype(F32)
    names = [info_ref[m].astype(F32) + 1.0 for m in range(PLANE)]
    count = backs[0].shape[0]
    _, _, hots = one_hots(names, half, count, side, routes)
    tails = joined(backs, half, width, width + LANES).astype(BF16)
    extra = jnp.zeros((side.shape[0], LANES), F32)
    first = lax.broadcasted_iota(jnp.int32, (count, 1), 0) < half
    for m in range(PLANE):
        hot = jnp.where(first if m % 2 == 0 else ~first, hots[m // 2], 0.0).astype(BF16)
        part = tails[m // 2 * count : (m // 2 + 1) * count]
        spread = lax.dot_general(hot, part, (((0,), (0,)), ((), ())), preferred_element_type=F32)
        extra = extra + jnp.where(side == names[m], spread, 0.0)
    picks = jnp.concatenate(hots, axis=0).astype(BF16)
    rows = joined(backs, half, 0, width).astype(BF16)
    total = lax.dot_general(picks, rows, (((0,), (0,)), ((), ())), preferred_element_type=F32)
    low = 0
    for out in outs:
        end = min(low + out.shape[1], width)
        out[:, : end - low] = total[:, low:end].astype(BF16)
        low = end
    outs[-1][:, outs[-1].shape[1] - LANES :] = extra.astype(BF16)


def add_kernel(*refs):
    out_ref, width, low, total = refs[-1], refs[-1].shape[1], 0, {}
    for r in refs[:-1]:
        total.setdefault((low, low + r.shape[1]), []).append(r[...].astype(F32))
        low = (low + r.shape[1]) % width
    whole = sum(total.pop((0, width)))
    out_ref[...] = whole
    for (low, end), values in total.items():
        out_ref[:, low:end] = whole[:, low:end] + sum(values)


def finish_kernel(routes, *refs):
    parts, (tokens_ref, combine_ref) = refs[:-2], refs[-2:]
    width = tokens_ref.shape[1]
    tokens_ref[...] = sum(r[:, :width].astype(F32) for r in parts).astype(BF16)
    side = sum(r[:, width:].astype(F32) for r in parts).T
    combine_ref[...] = side[:routes] + side[routes : 2 * routes]


def adapter_kernel(stages, half, rank, *refs):
    rows_in, refs = refs[: stages * PLANE], refs[stages * PLANE :]
    acts, lows, outs = refs[:stages], refs[stages : 2 * stages], refs[2 * stages :]
    width, hidden_units = outs[0].shape[2], outs[1].shape[2]

    def over_rows(part, other):
        return SCALE * lax.dot_general(part, other, (((0,), (0,)), ((), ())), preferred_element_type=F32)

    def every(low, high):
        pieces = [joined(rows_in[n * PLANE : (n + 1) * PLANE], half, low, high) for n in range(stages)]
        return jnp.concatenate(pieces, axis=0).astype(BF16)

    parts = [jnp.concatenate([r[:, n * LANES : (n + 1) * LANES] for r in lows], axis=0) for n in range(4)]
    act = [jnp.concatenate([r[:, n * hidden_units : (n + 1) * hidden_units] for r in acts], axis=0) for n in range(3)]
    by_x = over_rows(parts[0], every(0, width))
    outs[0][0] = by_x[:rank]
    outs[2][0] = by_x[rank : 2 * rank]
    outs[1][0] = over_rows(parts[1], act[1])[:rank]
    outs[3][0] = over_rows(parts[1], act[2])[rank : 2 * rank]
    outs[4][0] = over_rows(parts[2], act[0])[:rank]
    outs[5][0] = over_rows(parts[3], every(width, 2 * width))[:rank]


def on_device(tokens, grad_out, expert_ids, combine, *weights):
    rows, width = tokens.shape
    routes = expert_ids.shape[1]
    experts = lax.axis_size("expert")
    planes = experts // PLANE
    capacity = rows * routes * 9 // (8 * experts)
    pair = -(-2 * capacity // 8) * 8
    matrices = [w[0] for w in weights]
    hidden_units = matrices[0].shape[1]
    rank = matrices[3].shape[0]
    wide = width + LANES
    shape = jax.ShapeDtypeStruct

    me = lax.axis_index("expert").astype(jnp.int32)
    here, seat = me // PLANE, me % PLANE
    if planes == 4:
        end = ((here == 0) | (here == 3)).astype(jnp.int32)
        choice = [0 * end, 0 * end, end, end]
    else:
        offsets = [sorted({(p ^ n) - p for p in range(planes)}, key=lambda o: (abs(o), o)) for n in range(planes)]
        choice = [sum(jnp.where((here ^ n) - here == o, i, 0) for i, o in enumerate(offsets[n])) for n in range(planes)]
    info = jnp.stack([here * PLANE + (seat ^ m) for m in range(PLANE)] + choice).astype(jnp.int32)

    def along(value, step):
        pairs = [
            (p * PLANE + s, (p + step) * PLANE + s) for p in range(planes) for s in range(PLANE) if 0 <= p + step < planes
        ]
        return lax.ppermute(value, "expert", pairs)

    def flipped(value, mask, sources=range(planes)):
        pairs = [(p * PLANE + n, (p * PLANE + n) ^ mask) for p in sources for n in range(PLANE)]
        return lax.ppermute(value, "expert", pairs)

    def kernel(body, outs, args, micros, name, mib, scalars=0, where=pltpu.VMEM, scratch=()):
        vmem = pl.BlockSpec(memory_space=pltpu.VMEM)

        def run(*refs):
            given, rest = refs[: len(args)], refs[len(args) + len(last) :]
            rest[len(outs)][...] = jnp.zeros((8, LANES), F32)
            body(*given, *rest[: len(outs)], *rest[len(outs) + 1 :])

        *result, mark = pl.pallas_call(
            run,
            out_shape=[*outs, shape((8, LANES), F32)],
            in_specs=[smem()] * scalars
            + [pl.BlockSpec(memory_space=where)] * (len(args) - scalars)
            + [vmem] * len(last),
            out_specs=[vmem] * (len(outs) + 1),
            scratch_shapes=list(scratch),
            compiler_params=pltpu.CompilerParams(vmem_limit_bytes=mib * MIB),
            cost_estimate=pl.CostEstimate(flops=1, bytes_accessed=micros * RATE, transcendentals=0),
            name=name,
        )(*args, *last)
        last[:] = [mark]
        return result

    last = []
    (packed,) = kernel(
        functools.partial(pack_kernel, routes),
        [shape((rows, 2 * width + LANES), BF16)],
        (tokens, grad_out, expert_ids.T, combine.T),
        2,
        "pack",
        60,
        where=pltpu.HBM,
        scratch=(
            pltpu.VMEM((routes, rows), jnp.int32),
            pltpu.VMEM((routes, rows), F32),
            pltpu.SemaphoreType.DMA((4,)),
        ),
    )

    def expert(got):
        return kernel(
            functools.partial(expert_kernel, routes, capacity),
            [shape((pair, wide), BF16)] * 2
            + [shape((2 * pair, 3 * hidden_units), BF16), shape((2 * pair, 4 * LANES), BF16)],
            (*got, *adapters, *matrices[:3]),
            8,
            "expert",
            20,
        )

    def together(*values):
        *values, last[0] = lax.optimization_barrier((*values, last[0]))
        return values

    rows_of, sides, parts, acts, lows = {}, {}, {}, {}, {}

    def halfway(home, away):
        return home, flipped(home, 1), flipped(away, 2)

    def arrived(home, near, across):
        (across,) = together(across)
        return home, near, across, flipped(across, 1)

    def begin(stage, *found):
        *picked, sides[stage] = kernel(
            functools.partial(select_kernel, routes, capacity, len(found), stage),
            [shape((pair, 2 * width + LANES), BF16)] * 2 + [shape((rows, LANES), BF16)],
            (info, *found),
            4,
            "select",
            12,
            scalars=1,
        )
        rows_of[stage] = halfway(*picked)

    def middle_of(stage):
        rows_of[stage] = arrived(*rows_of[stage])
        *backs, acts[stage], lows[stage] = expert(rows_of[stage])
        parts[stage] = halfway(*backs)

    def end_of(stage, *columns):
        found = kernel(
            functools.partial(combine_kernel, routes, capacity),
            [shape((rows, c), BF16) for c in columns or (wide,)],
            (info, sides[stage], *arrived(*parts[stage])),
            3,
            "combine",
            8,
            scalars=1,
        )
        parts[stage] = [flipped(part, stage * PLANE) if stage else part for part in found]

    def add(*values):
        return kernel(add_kernel, [shape((rows, wide), F32)], values, 1, "add", 8)[0]

    adapters = []

    def prepare():
        adapters[:] = kernel(
            prepare_kernel,
            [
                shape((width, LANES), BF16),
                shape((LANES, width), BF16),
                shape((2, hidden_units, LANES), BF16),
                shape((2, LANES, hidden_units), BF16),
                shape((hidden_units, LANES), BF16),
                shape((LANES, hidden_units), BF16),
                shape((width, LANES), BF16),
            ],
            tuple(matrices[3:]),
            4,
            "prepare",
            8,
        )

    def adapter_sums():
        order = sorted(rows_of)
        return kernel(
            functools.partial(adapter_kernel, len(order), capacity, rank),
            [shape((1, rank, n), F32) for n in (width, hidden_units, width, hidden_units, hidden_units, width)],
            (*(r for n in order for r in rows_of[n]), *(acts[n] for n in order), *(lows[n] for n in order)),
            5,
            "adapter_grads",
            24,
        )

    if planes == 4:
        mids = (1, 2)
        mate, across = flipped(packed, PLANE), flipped(packed, 3 * PLANE, mids)
        begin(0, packed)
        prepare()
        mate, across = together(mate, across)
        mate_across, far = flipped(mate, 3 * PLANE, mids), flipped(across, PLANE)
        begin(1, mate)
        middle_of(0)
        mate_across, far = together(mate_across, far)
        farthest = flipped(mate_across, PLANE)
        begin(2, mate_across, far)
        middle_of(1)
        middle_of(2)
        (farthest,) = together(farthest)
        begin(3, across, farthest)
        first = width * 5 // (16 * LANES) * LANES
        end_of(2, first, wide - first)
        (parts[2][0],) = together(parts[2][0])
        middle_of(3)
        end_of(1)
        (parts[2][1],) = together(parts[2][1])
        end_of(3)
        grads = adapter_sums()
        end_of(0)
    else:
        blocks = {0: packed}
        for step in range(1, planes):
            for sign in (1, -1):
                blocks[sign * step] = along(blocks[sign * (step - 1)], -sign)
        prepare()
        for stage in range(planes):
            begin(stage, *(blocks[o] for o in offsets[stage]))
            middle_of(stage)
            end_of(stage)
        grads = adapter_sums()
    order = sorted(rows_of)
    total = add(*(part for n in order[:-1] for part in parts[n]))

    grad_tokens, grad_combine = kernel(
        functools.partial(finish_kernel, routes),
        [shape((rows, width), BF16), shape((routes, rows), F32)],
        (total, *parts[order[-1]]),
        3,
        "finish",
        8,
    )
    return (grad_tokens, grad_combine.T, *grads)


def solution(mesh):
    by_token = P(("groups", "expert"), None)
    by_part = P(("groups", "expert"), None, None)
    return jax.shard_map(
        on_device,
        mesh=mesh,
        in_specs=(by_token,) * 4 + (P("expert", None, None),) * 9,
        out_specs=(by_token,) * 2 + (by_part,) * 6,
        check_vma=False,
    )
```

```python
import functools

import jax
import jax.numpy as jnp
from jax import lax
from jax.experimental import pallas as pl
from jax.experimental.pallas import tpu as pltpu
from jax.sharding import PartitionSpec as P

SCALE = 2.0
PLANE = 4
LANES = 128
F32 = jnp.float32
BF16 = jnp.bfloat16
MIB = 1024 * 1024
RATE = 3000000


def nn(a, b):
    return lax.dot_general(a, b, (((1,), (0,)), ((), ())), preferred_element_type=F32)


def nt(a, b):
    return lax.dot_general(a, b, (((1,), (1,)), ((), ())), preferred_element_type=F32)


def two_parts(value):
    high = value.astype(BF16).astype(F32)
    return high, value - high


def smem():
    return pl.BlockSpec(memory_space=pltpu.SMEM)


def one_hots(names, half, rows, side, routes):
    turned = side.T
    tokens = side.shape[0]
    earlier = lax.broadcasted_iota(jnp.int32, (tokens, tokens), 0)
    later = lax.broadcasted_iota(jnp.int32, (tokens, tokens), 1)
    ahead = jnp.where(earlier < later, 1.0, 0.0).astype(BF16)
    place = lax.broadcasted_iota(jnp.int32, (rows, tokens), 0)
    every = [[jnp.where(turned[k : k + 1, :] == name, 1.0, 0.0) for k in range(routes)] for name in names]
    found = []
    for n, hits in enumerate(every):
        member = sum(hits)
        wide = jnp.broadcast_to(member, (8, tokens)).astype(BF16)
        slot = nn(wide, ahead)[0:1, :].astype(jnp.int32) + half * (n % 2)
        found.append(jnp.where((place == slot) & (member > 0.0), 1.0, 0.0))
    return turned, every, [found[n] + found[n + 1] for n in range(0, len(names), 2)]


def joined(refs, half, low, high):
    first = lax.broadcasted_iota(jnp.int32, (refs[0].shape[0], 1), 0) < half
    pieces = [r[:, low:high].astype(F32) for r in refs]
    return jnp.concatenate([jnp.where(first, pieces[n], pieces[n + 1]) for n in range(0, len(refs), 2)], axis=0)


def pack_kernel(routes, x_ref, grad_ref, ids_ref, weight_ref, out_ref, ids_buf, weight_buf, sems):
    tokens, width = grad_ref.shape
    targets = (out_ref.at[:, :width], out_ref.at[:, width : 2 * width], ids_buf, weight_buf)
    sources = (x_ref, grad_ref, ids_ref, weight_ref)
    copies = [pltpu.make_async_copy(a, b, sems.at[n]) for n, (a, b) in enumerate(zip(sources, targets))]
    for copy in copies:
        copy.start()
    copies[2].wait()
    copies[3].wait()
    names = ids_buf[...].astype(F32) + 1.0
    high, low = two_parts(weight_buf[...])
    row = lax.broadcasted_iota(jnp.int32, (LANES, tokens), 0)
    side = jnp.zeros((LANES, tokens), F32)
    for group, values in enumerate((names, names, high, low)):
        for k in range(routes):
            side = jnp.where(row == group * routes + k, values[k : k + 1, :], side)
    out_ref[:, 2 * width :] = side.T.astype(BF16)
    copies[0].wait()
    copies[1].wait()


def select_kernel(routes, half, choices, stage, info_ref, *refs):
    blocks, outs, side_ref = refs[:choices], refs[choices:-1], refs[-1]
    block = blocks[0][...]
    for i in range(1, choices):
        block = jnp.where(info_ref[PLANE + stage] == i, blocks[i][...], block)
    width = (block.shape[1] - LANES) // 2
    side_ref[...] = block[:, 2 * width :]
    side = block[:, 2 * width :].astype(F32)
    names = [info_ref[m].astype(F32) + 1.0 for m in range(PLANE)]
    turned, every, hots = one_hots(names, half, outs[0].shape[0], side, routes)
    lane = lax.broadcasted_iota(jnp.int32, (outs[0].shape[0], LANES), 1)
    chosen = nn(jnp.concatenate(hots, axis=0).astype(BF16), block[:, : 2 * width])
    rows = outs[0].shape[0]
    first = lax.broadcasted_iota(jnp.int32, (rows, 1), 0) < half
    for n, (hot, out) in enumerate(zip(hots, outs)):
        parts = []
        for group in (2, 3):
            weights = [
                sum(hits[k] * turned[group * routes + k : group * routes + k + 1, :] for k in range(routes))
                for hits in every[2 * n : 2 * n + 2]
            ]
            parts.append(jnp.sum(hot * jnp.where(first, weights[0], weights[1]), axis=1, keepdims=True))
        out[:, : 2 * width] = chosen[n * rows : (n + 1) * rows].astype(BF16)
        out[:, 2 * width :] = jnp.where(lane == 0, parts[0], jnp.where(lane == 1, parts[1], 0.0)).astype(BF16)


def prepare_kernel(gate_a, gate_b, up_a, up_b, down_a, down_b, *refs):
    def padded(*parts):
        rows, columns = sum(p.shape[0] for p in parts), parts[0].shape[1]
        return jnp.concatenate([*(p.astype(F32) for p in parts), jnp.zeros((LANES - rows, columns), F32)], axis=0)

    in_t, in_s, back_t, out_s, down_t, down_s, last_t = refs
    rank = gate_a.shape[0]
    both = padded(gate_a[...], up_a[...])
    in_t[...] = both.T.astype(BF16)
    in_s[...] = both.astype(BF16)
    gate = padded(gate_b[...])
    up = padded(jnp.zeros((rank, up_b.shape[1]), F32), up_b[...])
    out_s[0] = gate.astype(BF16)
    out_s[1] = up.astype(BF16)
    back_t[0] = gate.T.astype(BF16)
    back_t[1] = up.T.astype(BF16)
    down = padded(down_a[...])
    down_s[...] = down.astype(BF16)
    down_t[...] = down.T.astype(BF16)
    last_t[...] = padded(down_b[...]).T.astype(BF16)


def expert_kernel(routes, half, *refs):
    rows_in = refs[:PLANE]
    in_t, in_s, back_t, out_s, down_t, down_s, last_t, gate_w, up_w, down_w = refs[PLANE : PLANE + 10]
    *outs, acts_ref, lows_ref = refs[PLANE + 10 :]
    width, hidden_units = gate_w.shape
    x = joined(rows_in, half, 0, width).astype(BF16)
    g = joined(rows_in, half, width, 2 * width).astype(BF16)
    side = joined(rows_in, half, 2 * width, 2 * width + LANES)
    weight = side[:, 0:1] + side[:, 1:2]

    low = nn(x, in_t[...]).astype(BF16)
    g_low = nn(g, last_t[...])
    down_back = (weight * g_low).astype(BF16)
    gate_pre = nn(x, gate_w[...]) + SCALE * nn(low, out_s[0])
    up_pre = nn(x, up_w[...]) + SCALE * nn(low, out_s[1])
    q = jax.nn.sigmoid(gate_pre)
    silu = gate_pre * q
    hidden = (silu * up_pre).astype(BF16)
    low_down = nn(hidden, down_t[...]).astype(BF16).astype(F32)
    g_hidden = nt(g, down_w[...])
    dots = jnp.sum(hidden.astype(F32) * g_hidden, axis=1, keepdims=True)
    dots = dots + SCALE * jnp.sum(low_down * g_low, axis=1, keepdims=True)
    grad_hidden = weight * g_hidden + SCALE * nn(down_back, down_s[...])
    gate_grad = (grad_hidden * up_pre * q * (1.0 + gate_pre * (1.0 - q))).astype(BF16)
    up_grad = (grad_hidden * silu).astype(BF16)
    back = (nn(gate_grad, back_t[0]) + nn(up_grad, back_t[1])).astype(BF16)
    input_grad = nt(gate_grad, gate_w[...]) + nt(up_grad, up_w[...]) + SCALE * nn(back, in_s[...])
    high, lesser = two_parts(dots)
    lane = lax.broadcasted_iota(jnp.int32, (x.shape[0], LANES), 1)
    side_back = jnp.where(lane < routes, high, jnp.where(lane < 2 * routes, lesser, 0.0))
    rows = x.shape[0] // 2
    for n, out in enumerate(outs):
        out[:, :width] = input_grad[n * rows : (n + 1) * rows].astype(BF16)
        out[:, width:] = side_back[n * rows : (n + 1) * rows].astype(BF16)
    acts_ref[:, :hidden_units] = hidden
    acts_ref[:, hidden_units : 2 * hidden_units] = gate_grad
    acts_ref[:, 2 * hidden_units :] = up_grad
    for n, value in enumerate((back, low, down_back, (weight * low_down).astype(BF16))):
        lows_ref[:, n * LANES : (n + 1) * LANES] = value


def combine_kernel(routes, half, info_ref, side_ref, *refs):
    backs, outs = refs[:PLANE], refs[PLANE:]
    width = backs[0].shape[1] - LANES
    side = side_ref[...].astype(F32)
    names = [info_ref[m].astype(F32) + 1.0 for m in range(PLANE)]
    count = backs[0].shape[0]
    _, _, hots = one_hots(names, half, count, side, routes)
    tails = joined(backs, half, width, width + LANES).astype(BF16)
    extra = jnp.zeros((side.shape[0], LANES), F32)
    first = lax.broadcasted_iota(jnp.int32, (count, 1), 0) < half
    for m in range(PLANE):
        hot = jnp.where(first if m % 2 == 0 else ~first, hots[m // 2], 0.0).astype(BF16)
        part = tails[m // 2 * count : (m // 2 + 1) * count]
        spread = lax.dot_general(hot, part, (((0,), (0,)), ((), ())), preferred_element_type=F32)
        extra = extra + jnp.where(side == names[m], spread, 0.0)
    picks = jnp.concatenate(hots, axis=0).astype(BF16)
    rows = joined(backs, half, 0, width).astype(BF16)
    total = lax.dot_general(picks, rows, (((0,), (0,)), ((), ())), preferred_element_type=F32)
    low = 0
    for out in outs:
        end = min(low + out.shape[1], width)
        out[:, : end - low] = total[:, low:end].astype(BF16)
        low = end
    outs[-1][:, outs[-1].shape[1] - LANES :] = extra.astype(BF16)


def add_kernel(*refs):
    out_ref, width, low, total = refs[-1], refs[-1].shape[1], 0, {}
    for r in refs[:-1]:
        total.setdefault((low, low + r.shape[1]), []).append(r[...].astype(F32))
        low = (low + r.shape[1]) % width
    whole = sum(total.pop((0, width)))
    out_ref[...] = whole
    for (low, end), values in total.items():
        out_ref[:, low:end] = whole[:, low:end] + sum(values)


def finish_kernel(routes, *refs):
    parts, (tokens_ref, combine_ref) = refs[:-2], refs[-2:]
    width = tokens_ref.shape[1]
    tokens_ref[...] = sum(r[:, :width].astype(F32) for r in parts).astype(BF16)
    side = sum(r[:, width:].astype(F32) for r in parts).T
    combine_ref[...] = side[:routes] + side[routes : 2 * routes]


def adapter_kernel(stages, half, rank, *refs):
    rows_in, refs = refs[: stages * PLANE], refs[stages * PLANE :]
    acts, lows, outs = refs[:stages], refs[stages : 2 * stages], refs[2 * stages :]
    width, hidden_units = outs[0].shape[2], outs[1].shape[2]

    def over_rows(part, other):
        return SCALE * lax.dot_general(part, other, (((0,), (0,)), ((), ())), preferred_element_type=F32)

    def every(low, high):
        pieces = [joined(rows_in[n * PLANE : (n + 1) * PLANE], half, low, high) for n in range(stages)]
        return jnp.concatenate(pieces, axis=0).astype(BF16)

    parts = [jnp.concatenate([r[:, n * LANES : (n + 1) * LANES] for r in lows], axis=0) for n in range(4)]
    act = [jnp.concatenate([r[:, n * hidden_units : (n + 1) * hidden_units] for r in acts], axis=0) for n in range(3)]
    by_x = over_rows(parts[0], every(0, width))
    outs[0][0] = by_x[:rank]
    outs[2][0] = by_x[rank : 2 * rank]
    outs[1][0] = over_rows(parts[1], act[1])[:rank]
    outs[3][0] = over_rows(parts[1], act[2])[rank : 2 * rank]
    outs[4][0] = over_rows(parts[2], act[0])[:rank]
    outs[5][0] = over_rows(parts[3], every(width, 2 * width))[:rank]


def on_device(tokens, grad_out, expert_ids, combine, *weights):
    rows, width = tokens.shape
    routes = expert_ids.shape[1]
    experts = lax.axis_size("expert")
    planes = experts // PLANE
    capacity = rows * routes * 9 // (8 * experts)
    pair = -(-2 * capacity // 8) * 8
    matrices = [w[0] for w in weights]
    hidden_units = matrices[0].shape[1]
    rank = matrices[3].shape[0]
    wide = width + LANES
    shape = jax.ShapeDtypeStruct

    me = lax.axis_index("expert").astype(jnp.int32)
    here, seat = me // PLANE, me % PLANE
    if planes == 4:
        end = ((here == 0) | (here == 3)).astype(jnp.int32)
        choice = [0 * end, 0 * end, end, end]
    else:
        offsets = [sorted({(p ^ n) - p for p in range(planes)}, key=lambda o: (abs(o), o)) for n in range(planes)]
        choice = [sum(jnp.where((here ^ n) - here == o, i, 0) for i, o in enumerate(offsets[n])) for n in range(planes)]
    info = jnp.stack([here * PLANE + (seat ^ m) for m in range(PLANE)] + choice).astype(jnp.int32)

    def along(value, step):
        pairs = [
            (p * PLANE + s, (p + step) * PLANE + s) for p in range(planes) for s in range(PLANE) if 0 <= p + step < planes
        ]
        return lax.ppermute(value, "expert", pairs)

    def flipped(value, mask, sources=range(planes)):
        pairs = [(p * PLANE + n, (p * PLANE + n) ^ mask) for p in sources for n in range(PLANE)]
        return lax.ppermute(value, "expert", pairs)

    def kernel(body, outs, args, micros, name, mib, scalars=0, where=pltpu.VMEM, scratch=()):
        vmem = pl.BlockSpec(memory_space=pltpu.VMEM)

        def run(*refs):
            given, rest = refs[: len(args)], refs[len(args) + len(last) :]
            rest[len(outs)][...] = jnp.zeros((8, LANES), F32)
            body(*given, *rest[: len(outs)], *rest[len(outs) + 1 :])

        *result, mark = pl.pallas_call(
            run,
            out_shape=[*outs, shape((8, LANES), F32)],
            in_specs=[smem()] * scalars
            + [pl.BlockSpec(memory_space=where)] * (len(args) - scalars)
            + [vmem] * len(last),
            out_specs=[vmem] * (len(outs) + 1),
            scratch_shapes=list(scratch),
            compiler_params=pltpu.CompilerParams(vmem_limit_bytes=mib * MIB),
            cost_estimate=pl.CostEstimate(flops=1, bytes_accessed=micros * RATE, transcendentals=0),
            name=name,
        )(*args, *last)
        last[:] = [mark]
        return result

    last = []
    (packed,) = kernel(
        functools.partial(pack_kernel, routes),
        [shape((rows, 2 * width + LANES), BF16)],
        (tokens, grad_out, expert_ids.T, combine.T),
        2,
        "pack",
        60,
        where=pltpu.HBM,
        scratch=(
            pltpu.VMEM((routes, rows), jnp.int32),
            pltpu.VMEM((routes, rows), F32),
            pltpu.SemaphoreType.DMA((4,)),
        ),
    )

    def expert(got):
        return kernel(
            functools.partial(expert_kernel, routes, capacity),
            [shape((pair, wide), BF16)] * 2
            + [shape((2 * pair, 3 * hidden_units), BF16), shape((2 * pair, 4 * LANES), BF16)],
            (*got, *adapters, *matrices[:3]),
            8,
            "expert",
            20,
        )

    def together(*values):
        *values, last[0] = lax.optimization_barrier((*values, last[0]))
        return values

    rows_of, sides, parts, acts, lows = {}, {}, {}, {}, {}

    def halfway(home, away):
        return home, flipped(home, 1), flipped(away, 2)

    def arrived(home, near, across):
        (across,) = together(across)
        return home, near, across, flipped(across, 1)

    def begin(stage, *found):
        *picked, sides[stage] = kernel(
            functools.partial(select_kernel, routes, capacity, len(found), stage),
            [shape((pair, 2 * width + LANES), BF16)] * 2 + [shape((rows, LANES), BF16)],
            (info, *found),
            4,
            "select",
            12,
            scalars=1,
        )
        rows_of[stage] = halfway(*picked)

    def middle_of(stage):
        rows_of[stage] = arrived(*rows_of[stage])
        *backs, acts[stage], lows[stage] = expert(rows_of[stage])
        parts[stage] = halfway(*backs)

    def end_of(stage, *columns):
        found = kernel(
            functools.partial(combine_kernel, routes, capacity),
            [shape((rows, c), BF16) for c in columns or (wide,)],
            (info, sides[stage], *arrived(*parts[stage])),
            3,
            "combine",
            8,
            scalars=1,
        )
        parts[stage] = [flipped(part, stage * PLANE) if stage else part for part in found]

    def add(*values):
        return kernel(add_kernel, [shape((rows, wide), F32)], values, 1, "add", 8)[0]

    adapters = []

    def prepare():
        adapters[:] = kernel(
            prepare_kernel,
            [
                shape((width, LANES), BF16),
                shape((LANES, width), BF16),
                shape((2, hidden_units, LANES), BF16),
                shape((2, LANES, hidden_units), BF16),
                shape((hidden_units, LANES), BF16),
                shape((LANES, hidden_units), BF16),
                shape((width, LANES), BF16),
            ],
            tuple(matrices[3:]),
            4,
            "prepare",
            8,
        )

    def adapter_sums():
        order = sorted(rows_of)
        return kernel(
            functools.partial(adapter_kernel, len(order), capacity, rank),
            [shape((1, rank, n), F32) for n in (width, hidden_units, width, hidden_units, hidden_units, width)],
            (*(r for n in order for r in rows_of[n]), *(acts[n] for n in order), *(lows[n] for n in order)),
            5,
            "adapter_grads",
            24,
        )

    if planes == 4:
        mids = (1, 2)
        mate, across = flipped(packed, PLANE), flipped(packed, 3 * PLANE, mids)
        begin(0, packed)
        prepare()
        mate, across = together(mate, across)
        mate_across, far = flipped(mate, 3 * PLANE, mids), flipped(across, PLANE)
        begin(1, mate)
        middle_of(0)
        mate_across, far = together(mate_across, far)
        farthest = flipped(mate_across, PLANE)
        begin(2, mate_across, far)
        middle_of(1)
        middle_of(2)
        (farthest,) = together(farthest)
        begin(3, across, farthest)
        first = width * 5 // (16 * LANES) * LANES
        end_of(2, first, wide - first)
        (parts[2][0],) = together(parts[2][0])
        middle_of(3)
        end_of(1)
        (parts[2][1],) = together(parts[2][1])
        end_of(3)
        grads = adapter_sums()
        end_of(0)
    else:
        blocks = {0: packed}
        for step in range(1, planes):
            for sign in (1, -1):
                blocks[sign * step] = along(blocks[sign * (step - 1)], -sign)
        prepare()
        for stage in range(planes):
            begin(stage, *(blocks[o] for o in offsets[stage]))
            middle_of(stage)
            end_of(stage)
        grads = adapter_sums()
    order = sorted(rows_of)
    total = add(*(part for n in order[:-1] for part in parts[n]))

    grad_tokens, grad_combine = kernel(
        functools.partial(finish_kernel, routes),
        [shape((rows, width), BF16), shape((routes, rows), F32)],
        (total, *parts[order[-1]]),
        3,
        "finish",
        8,
    )
    return (grad_tokens, grad_combine.T, *grads)


def solution(mesh):
    by_token = P(("groups", "expert"), None)
    by_part = P(("groups", "expert"), None, None)
    return jax.shard_map(
        on_device,
        mesh=mesh,
        in_specs=(by_token,) * 4 + (P("expert", None, None),) * 9,
        out_specs=(by_token,) * 2 + (by_part,) * 6,
        check_vma=False,
    )
```
